256 devices in a mesh: ctx: 64 (over x, z, core), fsdp: 4 (over y).
Axes of the slice: x: 4, y: 4, z: 8, core: 2. Of those that a mesh axis runs over, the one named last changes fastest.
Arguments:
- query_rows: bfloat16 [8192, 2560], P('ctx', 'fsdp'), may hold values from -100 to 100
- key_rows: bfloat16 [8192, 512], P('ctx', 'fsdp'), may hold values from -4.5 to 4.5
- value_rows: bfloat16 [8192, 512], P('ctx', 'fsdp'), may hold values from -6 to 6
- mixed_grad: bfloat16 [8192, 2560], P('ctx', 'fsdp'), may hold values from -16 to 16
- layer_grad: bfloat16 [8192, 5120], P('ctx'), may hold values from -16 to 16
- state_feed: bfloat16 [8192, 4096], P('ctx', 'fsdp'), may hold values from -0.09375 to 0.09375
- write_map: bfloat16 [8192, 1024], P('ctx', 'fsdp'), may hold values from -0.25 to 0.25
- read_map: bfloat16 [8192, 1024], P('ctx', 'fsdp'), may hold values from -0.25 to 0.25
- log_decay: float32 [8192, 64], P('ctx', 'fsdp'), may hold values from -1 to 0
- scan_grad: bfloat16 [8192, 4096], P('ctx', 'fsdp'), may hold values from -6 to 6
Outputs:
- query_grad: bfloat16 [8192, 2560], P('ctx', 'fsdp')
- key_grad: bfloat16 [8192, 512], P('ctx', 'fsdp')
- value_grad: bfloat16 [8192, 512], P('ctx', 'fsdp')
- proj_grad: float32 [5120, 2560], P('ctx', 'fsdp')
- feed_grad: bfloat16 [8192, 4096], P('ctx', 'fsdp')
- write_grad: float32 [8192, 1024], P('ctx', 'fsdp')
- read_grad: float32 [8192, 1024], P('ctx', 'fsdp')
The draws below stay inside these ranges and needn't reach their ends.
All inputs are finite; a program needn't handle non-finite values.
Results may differ from the reference program's by a relative error of at most 0.023.
Values may be sent and summed in bfloat16 or wider, within the bound.
A program may use at most 256 MiB of HBM per device.

```python
import math
import jax
import jax.numpy as jnp
from jax import lax

D = 5120
HD = 128
KVH = 4
GROUPS = 5
QH = 20
LOCAL_STATE_HEADS = 64
SP = 64
NS = 128
NG = 8
TOK = 128
L = 8192
N_CTX = 64


def paired_rows(key):
    first_key, second_key = jax.random.split(key)
    sequence_length = TOK * N_CTX
    query_base = jnp.clip(jax.random.normal(first_key, (sequence_length, KVH * GROUPS * HD), jnp.float32), -4.5, 4.5)
    key_base = jnp.clip(jax.random.normal(second_key, (sequence_length, KVH * HD), jnp.float32), -4.5, 4.5)
    return (query_base, key_base)


def draw_key_rows(key, part):
    query_base, key_base = paired_rows(key)
    return key_base.astype(jnp.bfloat16)


def draw_query_rows(key, part):
    query_base, key_base = paired_rows(key)
    return query_base.astype(jnp.bfloat16)


def draw_log_decay(key, part):
    key = jax.random.fold_in(key, 3)
    divided_random_keys = jax.random.split(key, 6)
    sequence_length = TOK * N_CTX
    slow_count = 5
    keeping = jax.random.randint(divided_random_keys[0], (LOCAL_STATE_HEADS,), 0, 10) < slow_count
    slow_rate = jax.random.uniform(divided_random_keys[1], (LOCAL_STATE_HEADS,), jnp.float32, 0.2, 0.8) / sequence_length
    fast_rate = jax.random.uniform(divided_random_keys[2], (LOCAL_STATE_HEADS,), jnp.float32, 1.0 / 50.0, 1.0 / 30.0)
    decay_rate_floor = jnp.where(keeping, slow_rate, fast_rate)
    jitter_amplitude = jnp.exp(jax.random.uniform(divided_random_keys[3], (sequence_length, LOCAL_STATE_HEADS), jnp.float32, math.log(0.5), math.log(2.0)))
    spike_row_span = jax.random.randint(divided_random_keys[4], (sequence_length, 1), 0, sequence_length) < 3
    spike_loss_total = jax.random.uniform(divided_random_keys[5], (sequence_length, LOCAL_STATE_HEADS), jnp.float32, 0.2, 0.5)
    return -decay_rate_floor[None, :] * jitter_amplitude + jnp.where(spike_row_span, jnp.log(1.0 - spike_loss_total), 0.0)


def with_spikes(drawn, stream_key, source, target, parts, factor):
    def block_of(dim):
        return (jnp.arange(drawn.shape[dim]) // (drawn.shape[dim] // parts)).reshape((-1,) + (1,) * (drawn.ndim - 1 - dim))

    near = jax.random.permutation(stream_key, parts)[block_of(target)]
    far = (block_of(target) + parts // 2) % parts
    return jnp.where((block_of(source) == near) | (block_of(source) == far), factor * drawn, drawn)


def levels(stream_key, dims, cuts, least, high):
    gain = 1.0
    for axis_at, shards_of in cuts:
        draws = jax.random.uniform(jax.random.fold_in(jax.random.fold_in(stream_key, 6), axis_at), (shards_of,), jnp.float32, least / len(cuts), high / len(cuts))
        gain = gain * jnp.repeat(jnp.exp(draws), dims[axis_at] // shards_of).reshape((-1,) + (1,) * (len(dims) - 1 - axis_at))
    return gain


def scatter_about(key, extent, deviation, bound, pieces=(), held_as=jnp.bfloat16):
    loudness = levels(key, extent, pieces, -0.22, 0.18) if pieces else 1.0
    drawn = jax.random.normal(key, extent, jnp.float32) * deviation * loudness
    return jnp.minimum(jnp.maximum(drawn, -bound), bound).astype(held_as)


def noise_with(rng, shape, scale, bound, shards, heavy, kind=jnp.bfloat16):
    result = scale * jax.random.normal(rng, shape, jnp.float32)
    if shards:
        result = result * levels(rng, shape, shards, -0.22, 0.18)
    return jnp.clip(with_spikes(result, jax.random.fold_in(rng, 3), *heavy), -bound, bound).astype(kind)


def setup_inputs(seed: int = 0) -> dict:
    seeds = jax.random.split(jax.random.key(seed), 11)
    query_rows = draw_query_rows(jax.random.fold_in(seeds[10], 71), 0)
    key_rows = draw_key_rows(jax.random.fold_in(seeds[10], 71), 0)
    value_rows = scatter_about(seeds[2], (L, KVH * HD), 1.0, 6.0, ((0, 64), (1, 4)))
    mixed_grad = scatter_about(seeds[3], (L, QH * HD), 4.0, 16.0, ((0, 64), (1, 4)))
    layer_grad = noise_with(seeds[4], (L, D), 1.0, 16.0, ((0, 64),), (0, 1, 64, 4.0))
    state_feed = scatter_about(seeds[5], (L, LOCAL_STATE_HEADS * SP), ((LOCAL_STATE_HEADS // NG) * SP * (TOK * N_CTX) ** 0.5 / 10) ** -0.5, 0.09375, ((0, 64), (1, 4)))
    write_map = scatter_about(seeds[6], (L, NG * NS), (5 * (TOK * N_CTX) ** 0.5) ** -0.5, 0.25, ((0, 64), (1, 4)))
    read_map = scatter_about(seeds[7], (L, NG * NS), (5 * (TOK * N_CTX) ** 0.5) ** -0.5, 0.25, ((0, 64), (1, 4)))
    log_decay = draw_log_decay(jax.random.fold_in(seeds[10], 71), 0)
    scan_grad = scatter_about(seeds[9], (L, LOCAL_STATE_HEADS * SP), 1.0, 6.0, ((0, 64), (1, 4)))
    return dict(query_rows=query_rows, key_rows=key_rows, value_rows=value_rows, mixed_grad=mixed_grad, layer_grad=layer_grad, state_feed=state_feed, write_map=write_map, read_map=read_map, log_decay=log_decay, scan_grad=scan_grad)


HIGHEST = lax.Precision.HIGHEST
MASKED_SCORE = -1e30


def rounded(values):
    return lax.optimization_barrier(values.astype(jnp.bfloat16)).astype(jnp.float32)


def attention_backward(query_rows, key_rows, value_rows, mixed_grad):
    sequence_length = query_rows.shape[0]
    block_rows = 256 if sequence_length % 256 == 0 else sequence_length
    score_scale = HD ** -0.5
    query_heads = query_rows.astype(jnp.float32).reshape(sequence_length, KVH, GROUPS, HD)
    key_heads = key_rows.astype(jnp.float32).reshape(sequence_length, KVH, HD)
    value_heads = value_rows.astype(jnp.float32).reshape(sequence_length, KVH, HD)
    grad_heads = mixed_grad.astype(jnp.float32).reshape(sequence_length, KVH, GROUPS, HD)
    key_pos = jnp.arange(sequence_length, dtype=jnp.int32)

    def one_block(state_carry, block_index):
        key_acc, value_acc = state_carry
        first_row = (block_index * block_rows).astype(jnp.int32)
        queries = lax.dynamic_slice_in_dim(query_heads, first_row, block_rows, 0)
        grads = lax.dynamic_slice_in_dim(grad_heads, first_row, block_rows, 0)
        query_pos = first_row + jnp.arange(block_rows, dtype=jnp.int32)
        causal = key_pos[None, :] <= query_pos[:, None]
        scores = jnp.einsum("tkgd,skd->kgts", queries, key_heads, precision=HIGHEST) * score_scale
        masked = jnp.where(causal, scores, MASKED_SCORE)
        row_top = jnp.max(masked, axis=-1, keepdims=True)
        summed = jnp.sum(jnp.where(causal, jnp.exp(masked - row_top), 0.0), axis=-1, keepdims=True)
        log_total = row_top + jnp.log(summed)
        weights = jnp.where(causal, jnp.exp(masked - log_total), 0.0)
        weights16 = rounded(weights)
        attn_out = jnp.einsum("kgts,skd->tkgd", weights16, value_heads, precision=HIGHEST)
        row_delta = jnp.einsum("tkgd,tkgd->kgt", grads, attn_out, precision=HIGHEST)
        dweights = jnp.einsum("tkgd,skd->kgts", grads, value_heads, precision=HIGHEST)
        dscores = rounded(weights * (dweights - row_delta[..., None]))
        query_part = jnp.einsum("kgts,skd->tkgd", dscores, key_heads, precision=HIGHEST) * score_scale
        key_acc = key_acc + jnp.einsum("kgts,tkgd->skd", dscores, queries, precision=HIGHEST) * score_scale
        value_acc = value_acc + jnp.einsum("kgts,tkgd->skd", weights16, grads, precision=HIGHEST)
        return (key_acc, value_acc), (query_part.astype(jnp.bfloat16), attn_out.astype(jnp.bfloat16))

    zeros = jnp.zeros((sequence_length, KVH, HD), jnp.float32)
    blocks = jnp.arange(sequence_length // block_rows, dtype=jnp.int32)
    (key_acc, value_acc), (query_parts, mixed_parts) = lax.scan(one_block, (zeros, zeros), blocks)
    query_grad = query_parts.reshape(sequence_length, KVH * GROUPS * HD)
    mixed_out = mixed_parts.reshape(sequence_length, KVH * GROUPS * HD)
    key_grad = key_acc.reshape(sequence_length, KVH * HD).astype(jnp.bfloat16)
    value_grad = value_acc.reshape(sequence_length, KVH * HD).astype(jnp.bfloat16)
    return query_grad, key_grad, value_grad, mixed_out


def state_backward(state_feed, write_map, read_map, log_decay, scan_grad):
    sequence_length = state_feed.shape[0]
    group_size = LOCAL_STATE_HEADS // NG
    feed_rows = state_feed.astype(jnp.float32).reshape(sequence_length, LOCAL_STATE_HEADS, SP)
    grad_rows = scan_grad.astype(jnp.float32).reshape(sequence_length, LOCAL_STATE_HEADS, SP)
    write_heads = jnp.repeat(write_map.astype(jnp.float32).reshape(sequence_length, NG, NS), group_size, axis=1)
    read_heads = jnp.repeat(read_map.astype(jnp.float32).reshape(sequence_length, NG, NS), group_size, axis=1)

    def forward_step(states, inputs):
        decay_row, write_row, feed_row, grad_row = inputs
        states = jnp.exp(decay_row)[:, None, None] * states + write_row[:, :, None] * feed_row[:, None, :]
        return states, jnp.einsum("hnp,hp->hn", states, grad_row, precision=HIGHEST)

    empty = jnp.zeros((LOCAL_STATE_HEADS, NS, SP), jnp.float32)
    _, read_terms = lax.scan(forward_step, empty, (log_decay, write_heads, feed_rows, grad_rows))

    def backward_step(passed, inputs):
        decay_row, write_row, read_row, feed_row, grad_row = inputs
        back_states = read_row[:, :, None] * grad_row[:, None, :] + passed
        feed_part = jnp.einsum("hnp,hn->hp", back_states, write_row, precision=HIGHEST)
        write_part = jnp.einsum("hnp,hp->hn", back_states, feed_row, precision=HIGHEST)
        return jnp.exp(decay_row)[:, None, None] * back_states, (feed_part, write_part)

    _, (feed_parts, write_terms) = lax.scan(backward_step, empty, (log_decay, write_heads, read_heads, feed_rows, grad_rows), reverse=True)
    read_grad = read_terms.reshape(sequence_length, NG, group_size, NS).sum(axis=2).reshape(sequence_length, NG * NS)
    write_grad = write_terms.reshape(sequence_length, NG, group_size, NS).sum(axis=2).reshape(sequence_length, NG * NS)
    feed_grad = feed_parts.reshape(sequence_length, LOCAL_STATE_HEADS * SP).astype(jnp.bfloat16)
    return feed_grad, write_grad, read_grad


def reference(query_rows, key_rows, value_rows, mixed_grad, layer_grad, state_feed, write_map, read_map, log_decay, scan_grad):
    query_grad, key_grad, value_grad, mixed_out = attention_backward(query_rows, key_rows, value_rows, mixed_grad)
    proj_grad = jnp.dot(layer_grad.T, mixed_out, preferred_element_type=jnp.float32)
    feed_grad, write_grad, read_grad = state_backward(state_feed, write_map, read_map, log_decay, scan_grad)
    return (query_grad, key_grad, value_grad, proj_grad, feed_grad, write_grad, read_grad)
```

```python
import functools
import jax
import jax.numpy as jnp
from jax import lax
from jax.experimental import pallas as pl
from jax.experimental.pallas import tpu as pltpu
from jax.sharding import PartitionSpec as P

HD = 128
SP = 64
NS = 128
GROUPS = 5
ROWS = 128 * GROUPS
TK = 512
SCALE = HD ** (-0.5)
LOG2E = 1.4426950408889634
MESH = pl.DeviceIdType.MESH
F32 = jnp.float32
BF16 = jnp.bfloat16


def dot(a, b, ca, cb):
    return lax.dot_general(a, b, (((ca,), (cb,)), ((), ())), preferred_element_type=F32)


class Place:
    def __init__(self):
        self.me = lax.axis_index("ctx")
        self.y = lax.axis_index("fsdp")
        self.core = self.me % 2
        self.z = (self.me // 2) % 8
        self.x = self.me // 16

    def dev(self, x, z, core):
        return ((x * 8 + z) * 2 + core, self.y)


def add16(a, b):
    return (a.astype(F32) + b.astype(F32)).astype(BF16)


def att_kernel(q_ref, k_ref, v_ref, do_ref, dq_ref, dk_ref, dv_ref, mo_ref,
               kv, dkv, pst, qs, dot_ref, mst, l_ref, acc, sib,
               x1, x2, z1,
               ag_send, ag_recv, sib_recv, rs_send, rs_sib, rs_x, rs_z):
    p = Place()
    me, x, z, core = p.me, p.x, p.z, p.core
    other = 1 - core

    barrier = pltpu.get_barrier_semaphore()

    def greet(i, c):
        t = (me + i) % 64
        pl.semaphore_signal(barrier, inc=1, device_id=(t, p.y), device_id_type=MESH)
        return c

    lax.fori_loop(1, 64, greet, 0)
    kv[core, x, z, 0] = k_ref[...]
    kv[core, x, z, 1] = v_ref[...]
    pl.semaphore_wait(barrier, 63)

    def push(c, bx, bz, half, target):
        if half is None:
            src, sem = kv.at[c, bx, bz], ag_recv.at[bx, bz, 0]
        else:
            src, sem = kv.at[c, bx, bz, half], ag_recv.at[bx, bz, half]
        pltpu.make_async_remote_copy(
            src_ref=src, dst_ref=src, send_sem=ag_send, recv_sem=sem,
            device_id=target, device_id_type=MESH).start()

    def sibling(c, bx, bz):
        pltpu.make_async_remote_copy(
            src_ref=kv.at[c, bx, bz], dst_ref=kv.at[c, bx, bz], send_sem=ag_send,
            recv_sem=sib_recv.at[bx, bz], device_id=p.dev(x, z, 1 - c), device_id_type=MESH).start()

    def got(c, bx, bz, half=None):
        if half is None:
            ref, sem = kv.at[c, bx, bz], ag_recv.at[bx, bz, 0]
        else:
            ref, sem = kv.at[c, bx, bz, half], ag_recv.at[bx, bz, half]
        pltpu.make_async_remote_copy(
            src_ref=ref, dst_ref=ref, send_sem=ag_send, recv_sem=sem,
            device_id=p.dev(x, z, 1 - c), device_id_type=MESH).wait_recv()

    xr, xl, xo = (x + 1) % 4, (x + 3) % 4, (x + 2) % 4

    def zz(s):
        return (z + s + 8) % 8

    @pl.when(core == 0)
    def _():
        right, left = p.dev(x, zz(1), 0), p.dev(x, zz(-1), 0)
        xright, xleft = p.dev(xr, z, 0), p.dev(xl, z, 0)

        def spread(bz):
            push(0, x, bz, None, xright)
            push(0, x, bz, None, xleft)
            sibling(0, x, bz)

        def across(bz):
            got(0, xl, bz)
            push(0, xl, bz, 0, xright)
            sibling(0, xl, bz)
            got(0, xr, bz)
            push(0, xr, bz, 1, xleft)
            sibling(0, xr, bz)

        push(0, x, z, None, right)
        push(0, x, z, None, left)
        spread(z)
        for s in (1, 2, 3):
            got(0, x, zz(-s))
            push(0, x, zz(-s), None if s < 3 else 0, right)
            spread(zz(-s))
            got(0, x, zz(s))
            push(0, x, zz(s), None if s < 3 else 1, left)
            spread(zz(s))
            if s == 1:
                across(z)
            else:
                across(zz(1 - s))
                across(zz(s - 1))
        got(0, x, zz(4), 0)
        got(0, x, zz(4), 1)
        spread(zz(4))
        across(zz(-3))
        across(zz(3))
        across(zz(4))
        for s in (0, 1, -1, 2, -2, 3, -3, 4):
            got(0, xo, zz(s), 0)
            got(0, xo, zz(s), 1)
            sibling(0, xo, zz(s))

    @pl.when(core == 1)
    def _():
        right, left = p.dev(x, zz(1), 1), p.dev(x, zz(-1), 1)
        xright, xleft = p.dev(xr, z, 1), p.dev(xl, z, 1)

        def spread(bx):
            push(1, bx, z, None, right)
            push(1, bx, z, None, left)
            sibling(1, bx, z)

        push(1, x, z, None, xright)
        push(1, x, z, None, xleft)
        spread(x)
        got(1, xl, z)
        push(1, xl, z, 0, xright)
        spread(xl)
        got(1, xr, z)
        push(1, xr, z, 1, xleft)
        spread(xr)

        def along(bx, s):
            got(1, bx, zz(-s))
            push(1, bx, zz(-s), None if s < 3 else 0, right)
            sibling(1, bx, zz(-s))
            got(1, bx, zz(s))
            push(1, bx, zz(s), None if s < 3 else 1, left)
            sibling(1, bx, zz(s))

        along(x, 1)
        got(1, xo, z, 0)
        got(1, xo, z, 1)
        spread(xo)
        along(xl, 1)
        along(xr, 1)
        along(x, 2)
        along(xo, 1)
        along(xl, 2)
        along(xr, 2)
        along(x, 3)
        along(xo, 2)
        along(xl, 3)
        along(xr, 3)
        along(xo, 3)
        for bx in (x, xl, xr, xo):
            got(1, bx, zz(4), 0)
            got(1, bx, zz(4), 1)
            sibling(1, bx, zz(4))

    for g in range(GROUPS):
        cols = pl.ds(g * 128, 128)
        qs[g * 128:(g + 1) * 128, :] = q_ref[:, cols]
        dot_ref[:, cols] = do_ref[:, cols].astype(F32).T

    def zero(i, c):
        dkv[i // 32, (i // 8) % 4, i % 8] = jnp.zeros((2, 128, 128), BF16)
        return c

    lax.fori_loop(0, 64, zero, 0)
    acc[...] = jnp.zeros_like(acc)
    l_ref[...] = jnp.zeros_like(l_ref)

    def sib_wait(i, c):
        bx, bz = i // 8, i % 8
        pltpu.make_async_remote_copy(
            src_ref=kv.at[other, bx, bz], dst_ref=kv.at[other, bx, bz], send_sem=ag_send,
            recv_sem=sib_recv.at[bx, bz], device_id=p.dev(x, z, other), device_id_type=MESH).wait_recv()
        return c

    lax.fori_loop(0, 32, sib_wait, 0)
    whole = kv.at[0]
    part = kv.at[1, pl.ds(0, 3)]
    tail = kv.at[1, 3, pl.ds(0, 7)]
    for ref in (whole, part, tail):
        pltpu.make_async_copy(ref, ref, ag_send).wait()

    diag = me // 4

    def keys(j, which):
        return kv[:, j // 4, pl.ds(2 * (j % 4), 2), which].reshape(TK, HD)

    def forward(j, top, masked):
        s = dot(keys(j, 0), qs[...], 1, 1)
        if masked:
            row = lax.broadcasted_iota(jnp.int32, (TK, ROWS), 0)
            col = lax.broadcasted_iota(jnp.int32, (TK, ROWS), 1)
            pos = ((j * 4 + ((row // 128) % 2) * 2 + row // 256) * 128) + row % 128
            s = jnp.where(pos <= me * 128 + col % 128, s, -1e30)
        new = jnp.maximum(top, jnp.max(s, axis=0, keepdims=True))
        w = jnp.exp2((s - new) * (SCALE * LOG2E))
        shrink = jnp.exp2((top - new) * (SCALE * LOG2E))
        l_ref[...] = l_ref[...] * shrink + jnp.sum(w, axis=0, keepdims=True)
        w16 = w.astype(BF16)
        pst[j] = w16
        mst[j] = new
        acc[...] = acc[...] * shrink + dot(keys(j, 1), w16, 0, 0)
        return new

    top = lax.fori_loop(0, diag, lambda j, t: forward(j, t, False), jnp.full((1, ROWS), -1e30, F32))
    top = forward(diag, top, True)
    inv = 1.0 / l_ref[...]
    out_t = acc[...] * inv
    delta = jnp.sum(out_t * dot_ref[...], axis=0, keepdims=True)
    for g in range(GROUPS):
        mo_ref[:, g * 128:(g + 1) * 128] = out_t[:, g * 128:(g + 1) * 128].T.astype(BF16)
    acc[...] = jnp.zeros_like(acc)

    def backward(j, c):
        factor = jnp.exp2((mst[j] - top) * (SCALE * LOG2E)) * inv
        grad = (dot_ref[...] * factor).astype(BF16)
        dw = dot(keys(j, 1), grad, 1, 0)
        w16 = pst[j]
        ds = (w16.astype(F32) * (dw - delta * factor)).astype(BF16)
        dk = dot(ds, qs[...], 1, 0) * SCALE
        dv = dot(w16, grad, 1, 1)
        acc[...] = acc[...] + dot(keys(j, 0), ds, 0, 0)
        dkv[:, j // 4, pl.ds(2 * (j % 4), 2), 0] = dk.astype(BF16).reshape(2, 2, 128, 128)
        dkv[:, j // 4, pl.ds(2 * (j % 4), 2), 1] = dv.astype(BF16).reshape(2, 2, 128, 128)
        return c

    lax.fori_loop(0, diag + 1, backward, 0)
    for g in range(GROUPS):
        dq_ref[:, g * 128:(g + 1) * 128] = (acc[:, g * 128:(g + 1) * 128] * SCALE).T.astype(BF16)

    def remote(src, dst, sem, target):
        return pltpu.make_async_remote_copy(
            src_ref=src, dst_ref=dst, send_sem=rs_send, recv_sem=sem,
            device_id=target, device_id_type=MESH)

    for i in range(4):
        remote(dkv.at[other, i], sib.at[i], rs_sib.at[i], p.dev(x, z, other)).start()

    def sib_add(i, c):
        remote(dkv.at[other, i], sib.at[i], rs_sib.at[i], p.dev(x, z, other)).wait_recv()

        def one(b, c):
            dkv[core, i, b] = add16(dkv[core, i, b], sib[i, b])
            return c

        return lax.fori_loop(0, 8, one, c)

    lax.fori_loop(0, 4, sib_add, 0)

    @pl.when(core == 0)
    def _():
        xright, xleft = p.dev(xr, z, 0), p.dev(xl, z, 0)
        ra = remote(dkv.at[0, xo, :, 0], x1.at[0], rs_x.at[0, 0], xright)
        la = remote(dkv.at[0, xo, :, 1], x1.at[1], rs_x.at[0, 1], xleft)
        ra.start()
        la.start()
        ra.wait_recv()
        dkv[0, xr, :, 0] = add16(dkv[0, xr, :, 0], x1[0])
        rb = remote(dkv.at[0, xr], x2.at[0], rs_x.at[1, 0], xright)
        rb.start()
        la.wait_recv()
        dkv[0, xl, :, 1] = add16(dkv[0, xl, :, 1], x1[1])
        lb = remote(dkv.at[0, xl], x2.at[1], rs_x.at[1, 1], xleft)
        lb.start()
        rb.wait_recv()
        lb.wait_recv()

        def one(b, c):
            dkv[0, x, b] = (dkv[0, x, b].astype(F32) + x2[0, b].astype(F32) + x2[1, b].astype(F32)).astype(BF16)
            return c

        lax.fori_loop(0, 8, one, 0)
        right, left = p.dev(x, zz(1), 0), p.dev(x, zz(-1), 0)
        ra = remote(dkv.at[0, x, zz(4), 0], z1.at[0, 0, 0, 0], rs_z.at[0, 0], right)
        la = remote(dkv.at[0, x, zz(4), 1], z1.at[1, 0, 0, 1], rs_z.at[0, 1], left)
        ra.start()
        la.start()
        for s in (1, 2, 3):
            d = 4 - s
            ra.wait_recv()
            if s == 1:
                dkv[0, x, zz(d), 0] = add16(dkv[0, x, zz(d), 0], z1[0, 0, 0, 0])
            else:
                dkv[0, x, zz(d)] = add16(dkv[0, x, zz(d)], z1[0, s - 1, 0])
            ra = remote(dkv.at[0, x, zz(d)], z1.at[0, s, 0], rs_z.at[s, 0], right)
            ra.start()
            la.wait_recv()
            if s == 1:
                dkv[0, x, zz(-d), 1] = add16(dkv[0, x, zz(-d), 1], z1[1, 0, 0, 1])
            else:
                dkv[0, x, zz(-d)] = add16(dkv[0, x, zz(-d)], z1[1, s - 1, 0])
            la = remote(dkv.at[0, x, zz(-d)], z1.at[1, s, 0], rs_z.at[s, 1], left)
            la.start()
        ra.wait_recv()
        la.wait_recv()
        for ref, h in ((dk_ref, 0), (dv_ref, 1)):
            ref[...] = (dkv[0, x, z, h].astype(F32) + z1[0, 3, 0, h].astype(F32) + z1[1, 3, 0, h].astype(F32)).astype(BF16)

    @pl.when(core == 1)
    def _():
        right, left = p.dev(x, zz(1), 1), p.dev(x, zz(-1), 1)
        ra = remote(dkv.at[1, :, zz(4), 0], z1.at[0, 0, :, 0], rs_z.at[0, 0], right)
        la = remote(dkv.at[1, :, zz(4), 1], z1.at[1, 0, :, 1], rs_z.at[0, 1], left)
        ra.start()
        la.start()
        for s in (1, 2, 3):
            d = 4 - s
            ra.wait_recv()
            if s == 1:
                dkv[1, :, zz(d), 0] = add16(dkv[1, :, zz(d), 0], z1[0, 0, :, 0])
            else:
                dkv[1, :, zz(d)] = add16(dkv[1, :, zz(d)], z1[0, s - 1])
            ra = remote(dkv.at[1, :, zz(d)], z1.at[0, s], rs_z.at[s, 0], right)
            ra.start()
            la.wait_recv()
            if s == 1:
                dkv[1, :, zz(-d), 1] = add16(dkv[1, :, zz(-d), 1], z1[1, 0, :, 1])
            else:
                dkv[1, :, zz(-d)] = add16(dkv[1, :, zz(-d)], z1[1, s - 1])
            la = remote(dkv.at[1, :, zz(-d)], z1.at[1, s], rs_z.at[s, 1], left)
            la.start()
        ra.wait_recv()
        la.wait_recv()

        def one(b, c):
            dkv[1, b, z] = (dkv[1, b, z].astype(F32) + z1[0, 3, b].astype(F32) + z1[1, 3, b].astype(F32)).astype(BF16)
            return c

        lax.fori_loop(0, 4, one, 0)
        xright, xleft = p.dev(xr, z, 1), p.dev(xl, z, 1)
        ra = remote(dkv.at[1, xo, z, 0], x1.at[0, 0], rs_x.at[0, 0], xright)
        la = remote(dkv.at[1, xo, z, 1], x1.at[1, 0], rs_x.at[0, 1], xleft)
        ra.start()
        la.start()
        ra.wait_recv()
        dkv[1, xr, z, 0] = add16(dkv[1, xr, z, 0], x1[0, 0])
        rb = remote(dkv.at[1, xr, z], x2.at[0, 0], rs_x.at[1, 0], xright)
        rb.start()
        la.wait_recv()
        dkv[1, xl, z, 1] = add16(dkv[1, xl, z, 1], x1[1, 0])
        lb = remote(dkv.at[1, xl, z], x2.at[1, 0], rs_x.at[1, 1], xleft)
        lb.start()
        rb.wait_recv()
        lb.wait_recv()
        for ref, h in ((dk_ref, 0), (dv_ref, 1)):
            ref[...] = (dkv[1, x, z, h].astype(F32) + x2[0, 0, h].astype(F32) + x2[1, 0, h].astype(F32)).astype(BF16)

    for ref in (whole, part, tail):
        pltpu.make_async_copy(ref, ref, rs_send).wait()


def attention(query_rows, key_rows, value_rows, mixed_grad):
    vm = pl.BlockSpec(memory_space=pltpu.VMEM)
    dma = pltpu.SemaphoreType.DMA
    return pl.pallas_call(
        att_kernel,
        out_shape=(
            jax.ShapeDtypeStruct((128, ROWS), BF16),
            jax.ShapeDtypeStruct((128, 128), BF16),
            jax.ShapeDtypeStruct((128, 128), BF16),
            jax.ShapeDtypeStruct((128, ROWS), BF16),
        ),
        in_specs=[vm] * 4,
        out_specs=(vm,) * 4,
        scratch_shapes=[
            pltpu.VMEM((2, 4, 8, 2, 128, 128), BF16),
            pltpu.VMEM((2, 4, 8, 2, 128, 128), BF16),
            pltpu.VMEM((16, TK, ROWS), BF16),
            pltpu.VMEM((ROWS, HD), BF16),
            pltpu.VMEM((HD, ROWS), F32),
            pltpu.VMEM((16, 1, ROWS), F32),
            pltpu.VMEM((1, ROWS), F32),
            pltpu.VMEM((HD, ROWS), F32),
            pltpu.VMEM((4, 8, 2, 128, 128), BF16),
            pltpu.VMEM((2, 8, 128, 128), BF16),
            pltpu.VMEM((2, 8, 2, 128, 128), BF16),
            pltpu.VMEM((2, 4, 4, 2, 128, 128), BF16),
            dma,
            dma((4, 8, 2)),
            dma((4, 8)),
            dma,
            dma((4,)),
            dma((2, 2)),
            dma((4, 2)),
        ],
        compiler_params=pltpu.CompilerParams(
            collective_id=0, has_side_effects=True, vmem_limit_bytes=58 * 2**20
        ),
    )(query_rows, key_rows, value_rows, mixed_grad)


HIGHEST = lax.Precision.HIGHEST


def entering(part, axis, combine, identity, reverse):
    count = lax.axis_size(axis)
    place = lax.axis_index(axis)
    ahead = count - 1 - place if reverse else place
    gathered = jax.tree.map(lambda a: lax.all_gather(a, axis), part)
    state = jax.tree.map(lambda a, e: jnp.zeros_like(a) + jnp.asarray(e, a.dtype), part, identity)

    def one(hop, state):
        source = count - 1 - hop if reverse else hop
        return combine(
            state, jax.tree.map(lambda a: lax.dynamic_index_in_dim(a, source, 0, False), gathered)
        )

    return lax.fori_loop(0, ahead, one, state)


def chain_link(earlier, later):
    return (earlier[0] * later[0], later[0][:, None, None] * earlier[1] + later[1])


def per_device(
    query_rows,
    key_rows,
    value_rows,
    mixed_grad,
    layer_grad,
    state_feed,
    write_map,
    read_map,
    log_decay,
    scan_grad,
):
    tokens = query_rows.shape[0]
    query_grad, key_grad, value_grad, mixed_out = attention(query_rows, key_rows, value_rows, mixed_grad)
    proj_grad = lax.psum_scatter(
        lax.dot_general(
            layer_grad, mixed_out, (((0,), (0,)), ((), ())), preferred_element_type=jnp.float32
        ),
        "ctx",
        scatter_dimension=0,
        tiled=True,
    )
    ssm_heads = log_decay.shape[1]
    local_groups = write_map.shape[1] // NS
    group_size = ssm_heads // local_groups
    feed_narrow = state_feed.reshape(tokens, ssm_heads, SP)
    grad_narrow = scan_grad.reshape(tokens, ssm_heads, SP)
    write_narrow = jnp.repeat(write_map.reshape(tokens, local_groups, NS), group_size, axis=1)
    read_narrow = jnp.repeat(read_map.reshape(tokens, local_groups, NS), group_size, axis=1)
    feed_rows = feed_narrow.astype(jnp.float32)
    grad_rows = grad_narrow.astype(jnp.float32)
    write_heads = write_narrow.astype(jnp.float32)
    read_heads = read_narrow.astype(jnp.float32)
    running = jnp.cumsum(log_decay, axis=0)
    block_decay = running[-1]
    positions = jnp.arange(tokens, dtype=jnp.int32)
    earlier_mask = (positions[:, None] >= positions[None, :])[None]
    flipped = jnp.transpose(running)
    log_gaps = flipped[:, :, None] - flipped[:, None, :]
    decays = jnp.where(earlier_mask, jnp.exp(jnp.where(earlier_mask, log_gaps, 0.0)), 0.0)
    tail_decay = jnp.exp(block_decay[None, :] - running)
    head_decay = jnp.exp(running)
    local_state = jnp.einsum(
        "sh,shn,shp->hnp", tail_decay, write_heads, feed_rows, precision=HIGHEST
    )
    local_grad = jnp.einsum("sh,shn,shp->hnp", head_decay, read_heads, grad_rows, precision=HIGHEST)
    carried = jnp.exp(block_decay)
    identity_pair = (jnp.ones_like(carried), jnp.zeros_like(local_state))
    state_in = entering((carried, local_state), "ctx", chain_link, identity_pair, False)[1]
    grad_next = entering((carried, local_grad), "ctx", chain_link, identity_pair, True)[1]
    cross_terms = jnp.einsum(
        "ahp,bhp->hab", grad_narrow, feed_narrow, preferred_element_type=jnp.float32
    )
    inner_terms = decays * cross_terms
    read_term = jnp.einsum(
        "th,hnp,thp->thn", head_decay, state_in, grad_rows, precision=HIGHEST
    ) + jnp.einsum("htb,bhn->thn", inner_terms, write_heads, precision=HIGHEST)
    write_term = jnp.einsum(
        "hat,ahn->thn", inner_terms, read_heads, precision=HIGHEST
    ) + jnp.einsum("th,hnp,thp->thn", tail_decay, grad_next, feed_rows, precision=HIGHEST)
    pairing = jnp.einsum(
        "thn,shn->hts", write_narrow, read_narrow, preferred_element_type=jnp.float32
    )
    feed_full = jnp.einsum(
        "hst,hts,shp->thp", decays, pairing, grad_rows, precision=HIGHEST
    ) + jnp.einsum("th,thn,hnp->thp", tail_decay, write_heads, grad_next, precision=HIGHEST)
    feed_grad = feed_full.reshape(tokens, ssm_heads * SP).astype(jnp.bfloat16)
    read_grad = (
        read_term.reshape(tokens, local_groups, group_size, NS)
        .sum(axis=2)
        .reshape(tokens, local_groups * NS)
    )
    write_grad = (
        write_term.reshape(tokens, local_groups, group_size, NS)
        .sum(axis=2)
        .reshape(tokens, local_groups * NS)
    )
    return (query_grad, key_grad, value_grad, proj_grad, feed_grad, write_grad, read_grad)


def solution(mesh):
    return jax.shard_map(
        per_device,
        mesh=mesh,
        in_specs=(
            P("ctx", "fsdp"),
            P("ctx", "fsdp"),
            P("ctx", "fsdp"),
            P("ctx", "fsdp"),
            P("ctx", None),
            P("ctx", "fsdp"),
            P("ctx", "fsdp"),
            P("ctx", "fsdp"),
            P("ctx", "fsdp"),
            P("ctx", "fsdp"),
        ),
        out_specs=(
            P("ctx", "fsdp"),
            P("ctx", "fsdp"),
            P("ctx", "fsdp"),
            P("ctx", "fsdp"),
            P("ctx", "fsdp"),
            P("ctx", "fsdp"),
            P("ctx", "fsdp"),
        ),
        check_vma=False,
    )
```

```python
import functools
import jax
import jax.numpy as jnp
from jax import lax
from jax.experimental import pallas as pl
from jax.experimental.pallas import tpu as pltpu
from jax.sharding import PartitionSpec as P

HD = 128
NS = 128
HALF = 512
COLS = 1280
GROUPS = 5
ROWS = 128 * GROUPS
TK = 512
SCALE = HD ** (-0.5)
LOG2E = 1.4426950408889634
MESH = pl.DeviceIdType.MESH
F32 = jnp.float32
BF16 = jnp.bfloat16


def dot(a, b, ca, cb):
    return lax.dot_general(a, b, (((ca,), (cb,)), ((), ())), preferred_element_type=F32)


class Place:
    def __init__(self):
        self.me = lax.axis_index("ctx")
        self.y = lax.axis_index("fsdp")
        self.core = self.me % 2
        self.z = (self.me // 2) % 8
        self.x = self.me // 16

    def dev(self, x, z, core):
        return ((x * 8 + z) * 2 + core, self.y)

    def across(self, step):
        return (self.me, (self.y + step) % 4)


def exact(a, b):
    return lax.dot_general(
        a, b, (((1,), (0,)), ((), ())), preferred_element_type=F32, precision=lax.Precision.HIGHEST
    )


def add16(a, b):
    return (a.astype(F32) + b.astype(F32)).astype(BF16)


def in_turns(order, *steps):
    for i in order:
        next(steps[i], None)
    for step in steps:
        for _ in step:
            pass


def kernel(q_ref, k_ref, v_ref, do_ref, lg_ref, f_ref, w_ref, r_ref, ld_ref, g_ref,
           dq_ref, dk_ref, dv_ref, pg_ref, feed_ref, write_ref, read_ref,
           kv, dkv, pst, qs, dot_ref, mst, l_ref, top_ref, acc, sib,
           x1, x2, z1, xin, zin,
           mo4, lg4, pj, psib, pz,
           lds, a_ref, at_ref, tx, fw, gh, fed, inner,
           mine_s, sx, sy, lt, ls, t16, cdl, in1, xt, out2, in2, vx, vy, si, gn,
           ag_send, ag_recv, sib_recv, rs_send, rs_sib_send, rs_sib, rs_x, rs_z, rs_xin, rs_zin,
           mo_send, mo_recv, lg_send, lg_recv, lg_own, lg_y, pj_send, pj_sib, pj_z,
           s_pair, s_z, s_x, s_back, s_last):
    p = Place()
    me, x, z, core = p.me, p.x, p.z, p.core
    other = 1 - core

    barrier = pltpu.get_barrier_semaphore()

    def zz(s):
        return (z + s + 8) % 8

    xr, xl, xo = (x + 1) % 4, (x + 3) % 4, (x + 2) % 4
    partners = [p.dev(x, z, other)] + [p.dev(t, z, core) for t in (xr, xl, xo)]
    partners += [p.dev(x, zz(i), core) for i in range(1, 8)]
    partners += [p.across(1), p.across(3)]
    for t in partners:
        pl.semaphore_signal(barrier, inc=1, device_id=t, device_id_type=MESH)
    kv[core, x, z, 0] = k_ref[...]
    kv[core, x, z, 1] = v_ref[...]
    pl.semaphore_wait(barrier, 13)

    def push(c, bx, bz, half, target):
        if half is None:
            src, sem = kv.at[c, bx, bz], ag_recv.at[bx, bz, 0]
        else:
            src, sem = kv.at[c, bx, bz, half], ag_recv.at[bx, bz, half]
        pltpu.make_async_remote_copy(
            src_ref=src, dst_ref=src, send_sem=ag_send, recv_sem=sem,
            device_id=target, device_id_type=MESH).start()

    def sibling(c, bx, bz):
        pltpu.make_async_remote_copy(
            src_ref=kv.at[c, bx, bz], dst_ref=kv.at[c, bx, bz], send_sem=ag_send,
            recv_sem=sib_recv.at[bx, bz], device_id=p.dev(x, z, 1 - c), device_id_type=MESH).start()

    def got(c, bx, bz, half=None):
        if half is None:
            ref, sem = kv.at[c, bx, bz], ag_recv.at[bx, bz, 0]
        else:
            ref, sem = kv.at[c, bx, bz, half], ag_recv.at[bx, bz, half]
        pltpu.make_async_remote_copy(
            src_ref=ref, dst_ref=ref, send_sem=ag_send, recv_sem=sem,
            device_id=p.dev(x, z, 1 - c), device_id_type=MESH).wait_recv()

    @pl.when(core == 0)
    def _():
        push(0, x, z, None, p.dev(x, zz(1), 0))
        push(0, x, z, None, p.dev(x, zz(-1), 0))
        push(0, x, z, None, p.dev(xr, z, 0))
        push(0, x, z, None, p.dev(xl, z, 0))
        sibling(0, x, z)

    @pl.when(core == 1)
    def _():
        push(1, x, z, None, p.dev(xr, z, 1))
        push(1, x, z, None, p.dev(xl, z, 1))
        push(1, x, z, None, p.dev(x, zz(1), 1))
        push(1, x, z, None, p.dev(x, zz(-1), 1))
        sibling(1, x, z)

    for g in range(GROUPS):
        cols = pl.ds(g * 128, 128)
        qs[g * 128:(g + 1) * 128, :] = q_ref[:, cols]
        dot_ref[:, cols] = do_ref[:, cols].astype(F32).T

    def zero(i, c):
        dkv[i // 32, (i // 8) % 4, i % 8] = jnp.zeros((2, 128, 128), BF16)
        return c

    lax.fori_loop(0, 64, zero, 0)
    acc[...] = jnp.zeros_like(acc)
    l_ref[...] = jnp.zeros_like(l_ref)
    top_ref[...] = jnp.full_like(top_ref, -1e30)

    def pair_copy(src, dst, i):
        return pltpu.make_async_remote_copy(
            src_ref=src, dst_ref=dst, send_sem=s_pair.at[i, 0], recv_sem=s_pair.at[i, 1],
            device_id=p.dev(x, z, other), device_id_type=MESH)

    def states_alone():
        row = lax.broadcasted_iota(jnp.int32, (128, 128), 0)
        col = lax.broadcasted_iota(jnp.int32, (128, 128), 1)
        lds[...] = jnp.zeros_like(lds)
        lds[0:16, :] = ld_ref[...]
        running = exact((row >= col).astype(F32), lds[...].T)
        a_ref[...] = running
        at_ref[...] = running.T
        total = running[127:128, :]
        spread_heads = (
            lax.broadcasted_iota(jnp.int32, (128, 1024), 1) // 64
            == lax.broadcasted_iota(jnp.int32, (128, 1024), 0)
        ).astype(F32)
        tx[...] = exact(jnp.exp(total - running), spread_heads)
        fw[...] = (f_ref[...].astype(F32) * tx[...]).astype(BF16)
        gh[...] = (g_ref[...].astype(F32) * exact(jnp.exp(running), spread_heads)).astype(BF16)
        lt[...] = exact(jnp.broadcast_to(total, (8, 128)), spread_heads)
        for g in range(2):
            wide = slice(g * HALF, (g + 1) * HALF)
            narrow = slice(g * NS, (g + 1) * NS)
            state = dot(w_ref[:, narrow], fw[:, wide], 0, 0)
            back = dot(r_ref[:, narrow], gh[:, wide], 0, 0)

            @pl.when(core == 0)
            def _():
                mine_s[:, wide] = state
                sx[:, wide] = back.astype(BF16)

            @pl.when(core == 1)
            def _():
                mine_s[:, wide] = back
                sx[:, wide] = state.astype(BF16)

        pair_copy(sx, sy, 0).start()
        pair_copy(lt, ls, 1).start()
        yield
        low_half = col < 64

        def two(value):
            full = value.astype(F32)
            return jnp.concatenate(
                [jnp.where(low_half, full, 0.0), jnp.where(low_half, 0.0, full)], axis=0
            ).astype(BF16)

        for g in range(2):
            narrow = slice(g * NS, (g + 1) * NS)
            pairing = dot(w_ref[:, narrow], r_ref[:, narrow], 1, 1)
            inner[...] = jnp.zeros_like(inner)
            for k in range(4):
                lanes = slice(g * HALF + k * 128, g * HALF + (k + 1) * 128)
                head = g * 8 + 2 * k
                decays = []
                for h in (head, head + 1):
                    gap = at_ref[h:h + 1, :] - a_ref[:, h:h + 1]
                    decays.append(jnp.where(col >= row, jnp.exp(jnp.where(col >= row, gap, 0.0)), 0.0))
                grads = g_ref[:, lanes]
                cross = dot(two(f_ref[:, lanes]), grads, 1, 1)
                inner[...] += decays[0] * cross[0:128] + decays[1] * cross[128:256]
                mixed = jnp.concatenate([d * pairing for d in decays], axis=1).astype(BF16)
                fed[:, lanes] = dot(mixed, two(grads), 1, 0)
                yield
            inner16 = inner[...].astype(BF16)
            write_ref[:, narrow] = dot(inner16, r_ref[:, narrow], 1, 0)
            read_ref[:, narrow] = dot(inner16, w_ref[:, narrow], 0, 0)

    right, left = p.dev(x, zz(1), core), p.dev(x, zz(-1), core)
    xright, xleft = p.dev(xr, z, core), p.dev(xl, z, core)

    def spread_x(bz):
        push(0, x, bz, None, xright)
        push(0, x, bz, None, xleft)
        sibling(0, x, bz)

    def across(bz):
        got(0, xl, bz)
        push(0, xl, bz, 0, xright)
        sibling(0, xl, bz)
        got(0, xr, bz)
        push(0, xr, bz, 1, xleft)
        sibling(0, xr, bz)

    def opposite(bz):
        got(0, xo, bz, 0)
        got(0, xo, bz, 1)
        sibling(0, xo, bz)

    def row_step(s):
        got(0, x, zz(-s))
        push(0, x, zz(-s), None if s < 3 else 0, right)
        spread_x(zz(-s))
        got(0, x, zz(s))
        push(0, x, zz(s), None if s < 3 else 1, left)
        spread_x(zz(s))

    def spread_z(bx):
        push(1, bx, z, None, right)
        push(1, bx, z, None, left)
        sibling(1, bx, z)

    def along(bx, s):
        got(1, bx, zz(-s))
        push(1, bx, zz(-s), None if s < 3 else 0, right)
        sibling(1, bx, zz(-s))
        got(1, bx, zz(s))
        push(1, bx, zz(s), None if s < 3 else 1, left)
        sibling(1, bx, zz(s))

    def first(k):
        if k == 0:
            row_step(1)
        elif k == 1:
            across(z)
            row_step(2)
        elif k == 2:
            across(zz(-1))
            across(zz(1))
            opposite(z)
            row_step(3)
        elif k == 3:
            opposite(zz(-1))
            opposite(zz(1))
            across(zz(-2))
            across(zz(2))
            got(0, x, zz(4), 0)
            got(0, x, zz(4), 1)
            spread_x(zz(4))
        elif k == 4:
            across(zz(-3))
            across(zz(3))
            opposite(zz(-2))
            opposite(zz(2))
        elif k == 5:
            across(zz(4))
            opposite(zz(-3))
            opposite(zz(3))
        else:
            opposite(zz(4))

    def second(k):
        if k == 0:
            got(1, xl, z)
            push(1, xl, z, 0, xright)
            spread_z(xl)
            got(1, xr, z)
            push(1, xr, z, 1, xleft)
            spread_z(xr)
            along(x, 1)
        elif k == 1:
            got(1, xo, z, 0)
            got(1, xo, z, 1)
            spread_z(xo)
            along(xl, 1)
            along(xr, 1)
        elif k == 2:
            along(x, 2)
            along(xo, 1)
        elif k == 3:
            along(xl, 2)
            along(xr, 2)
            along(x, 3)
            along(xo, 2)
        elif k == 4:
            along(xl, 3)
            along(xr, 3)
            along(xo, 3)
        elif k == 5:
            for bx in (x, xl):
                got(1, bx, zz(4), 0)
                got(1, bx, zz(4), 1)
                sibling(1, bx, zz(4))
        else:
            for bx in (xr, xo):
                got(1, bx, zz(4), 0)
                got(1, bx, zz(4), 1)
                sibling(1, bx, zz(4))

    def gather(k):
        @pl.when(core == 0)
        def _():
            first(k)

        @pl.when(core == 1)
        def _():
            second(k)

    def order(k, n):
        return k + core * (n - 1 - 2 * k)

    def z_copy(i, src, dst, sems, slot):
        t = zz(i)
        return pltpu.make_async_remote_copy(
            src_ref=src.at[slot(t)], dst_ref=dst.at[z], send_sem=sems.at[0, i], recv_sem=sems.at[1, z],
            device_id=p.dev(x, t, core), device_id_type=MESH)

    def z_wait(i, src, dst, sems, slot):
        t = zz(i)
        pltpu.make_async_remote_copy(
            src_ref=src.at[slot(t)], dst_ref=dst.at[t], send_sem=sems.at[0, i], recv_sem=sems.at[1, t],
            device_id=p.dev(x, t, core), device_id_type=MESH).wait()

    def at_target(t):
        return t

    def at_home(t):
        return z

    def states_join():
        pair_copy(sx, sy, 0).wait()
        pair_copy(lt, ls, 1).wait()
        joined = jnp.exp(ls[0:1, :]) * mine_s[...] + sy[...].astype(F32)
        t16[...] = joined.astype(BF16).reshape(8, 16, 1024)
        cdl[z] = lt[...] + ls[...]
        for i in range(1, 8):
            z_copy(i, t16, in1, s_z.at[0], at_target).start()
            z_copy(i, cdl, cdl, s_z.at[1], at_home).start()
        in1[z] = t16[z]

    def x_copy(i, t):
        return pltpu.make_async_remote_copy(
            src_ref=xt.at[i], dst_ref=xt.at[i], send_sem=s_x.at[0, (t - x + 4) % 4], recv_sem=s_x.at[1, i],
            device_id=p.dev(t, z, core), device_id_type=MESH)

    def along_row(state, keep):
        for k in range(8):
            c = order(k, 8)
            if keep:
                out2[c] = state.astype(BF16)
            state = jnp.exp(cdl[c, 0:1, :]) * state + in1[c].astype(F32)
        return state

    def states_row():
        for i in range(1, 8):
            z_wait(i, t16, in1, s_z.at[0], at_target)
            z_wait(i, cdl, cdl, s_z.at[1], at_home)
        xt[x, 0:16, :] = along_row(jnp.zeros((16, 1024), F32), False)
        summed = cdl[0]
        for k in range(1, 8):
            summed = summed + cdl[k]
        xt[x, 16:24, :] = summed
        for t in (xr, xl, xo):
            x_copy(x, t).start()

    def states_back():
        for t in (xr, xl, xo):
            x_copy(x, t).wait_send()
            x_copy(t, t).wait_recv()
        state = jnp.zeros((16, 1024), F32)
        mine_at = order(0, 4) + x - 2 * core * x
        for k in range(3):
            c = order(k, 4)
            later = jnp.exp(xt[c, 16:17, :]) * state + xt[c, 0:16, :]
            state = jnp.where(k < mine_at, later, state)
        along_row(state, True)
        for i in range(1, 8):
            z_copy(i, out2, in2, s_back, at_target).start()
        in2[z] = out2[z]

    def states_last():
        for i in range(1, 8):
            z_wait(i, out2, in2, s_back, at_target)
        entered = in2[...].reshape(128, 1024)
        vx[...] = (jnp.exp(lt[0:1, :]) * entered.astype(F32) + mine_s[...]).astype(BF16)
        pair_copy(vx, vy, 2).start()

    def columns(i):
        return pl.ds(pl.multiple_of(i * COLS, 128), COLS)

    def quarter(y):
        return pl.ds(pl.multiple_of(((y + 4) % 4) * 32, 32), 32)

    def lg_copy(i, t):
        return pltpu.make_async_remote_copy(
            src_ref=lg_ref.at[quarter(p.y), columns(t)], dst_ref=lg4.at[i, quarter(p.y)],
            send_sem=lg_send, recv_sem=lg_recv.at[i],
            device_id=p.dev(t, z, core), device_id_type=MESH)

    def lg_turn(step):
        ref = lg4.at[:, quarter(p.y)]
        return pltpu.make_async_remote_copy(
            src_ref=ref, dst_ref=ref, send_sem=lg_y.at[0, step // 2], recv_sem=lg_y.at[1, step // 2],
            device_id=p.across(step), device_id_type=MESH)

    def lg_from(step):
        ref = lg4.at[:, quarter(p.y + step)]
        return pltpu.make_async_remote_copy(
            src_ref=ref, dst_ref=ref, send_sem=lg_y.at[0, 0], recv_sem=lg_y.at[1, 1 - step // 2],
            device_id=p.across(step), device_id_type=MESH)

    def lg_pass(step, y):
        ref = lg4.at[pl.ds(step - 1, 2), quarter(y)]
        return pltpu.make_async_remote_copy(
            src_ref=ref, dst_ref=ref, send_sem=lg_y.at[0, 2 + step // 2], recv_sem=lg_y.at[1, 2 + step // 2],
            device_id=p.across(step), device_id_type=MESH)

    def mo_copy(i, t):
        return pltpu.make_async_remote_copy(
            src_ref=mo4.at[i], dst_ref=mo4.at[i], send_sem=mo_send, recv_sem=mo_recv.at[i],
            device_id=p.dev(t, z, core), device_id_type=MESH)

    lg_mine = pltpu.make_async_copy(
        lg_ref.at[quarter(p.y), columns(x)], lg4.at[x, quarter(p.y)], lg_own)
    lg_mine.start()
    for t in (xr, xl, xo):
        lg_copy(x, t).start()

    diag = me // 4
    zp = z // 2

    def keys(j, which):
        return kv[:, j // 4, pl.ds(2 * (j % 4), 2), which].reshape(TK, HD)

    def forward(j, masked):
        top = top_ref[...]
        s = dot(keys(j, 0), qs[...], 1, 1)
        if masked:
            r = lax.broadcasted_iota(jnp.int32, (TK, ROWS), 0)
            c = lax.broadcasted_iota(jnp.int32, (TK, ROWS), 1)
            pos = ((j * 4 + ((r // 128) % 2) * 2 + r // 256) * 128) + r % 128
            s = jnp.where(pos <= me * 128 + c % 128, s, -1e30)
        new = jnp.maximum(top, jnp.max(s, axis=0, keepdims=True))
        w = jnp.exp2((s - new) * (SCALE * LOG2E))
        shrink = jnp.exp2((top - new) * (SCALE * LOG2E))
        l_ref[...] = l_ref[...] * shrink + jnp.sum(w, axis=0, keepdims=True)
        w16 = w.astype(BF16)
        pst[j] = w16
        mst[j] = new
        top_ref[...] = new
        acc[...] = acc[...] * shrink + dot(keys(j, 1), w16, 0, 0)

    def sib_wait(bx, bz):
        pltpu.make_async_remote_copy(
            src_ref=kv.at[other, bx, bz], dst_ref=kv.at[other, bx, bz], send_sem=ag_send,
            recv_sem=sib_recv.at[bx, bz], device_id=p.dev(x, z, other), device_id_type=MESH).wait_recv()

    def column_ready(i):
        c = (zp + i) % 4

        def one(b, carry):
            sib_wait(b // 2, 2 * c + b % 2)
            return carry

        lax.fori_loop(0, 8, one, 0)

    def column(i, start, stop):
        c = (zp + i) % 4

        def one(b, carry):
            forward(4 * b + c, False)
            return carry

        lax.fori_loop(start, jnp.minimum(stop, (diag - c + 3) // 4), one, 0)

    alone = states_alone()
    next(alone)
    gather(0)
    next(alone)
    next(alone)
    gather(1)
    next(alone)
    next(alone)
    gather(2)
    next(alone)
    next(alone)
    gather(3)
    for _ in alone:
        pass
    lg_mine.wait()
    for t in (xr, xl, xo):
        lg_copy(t, t).wait_recv()
    lg_turn(1).start()
    lg_turn(3).start()
    column_ready(0)
    forward(diag, True)
    gather(4)
    column(0, 0, 4)
    states_join()
    gather(5)
    column_ready(1)
    column_ready(3)
    column(1, 0, 4)
    gather(6)
    for step in (1, 3):
        lg_from(step).wait_recv()
    lg_pass(1, p.y - 1).start()
    lg_pass(3, p.y + 1).start()
    column(3, 0, 4)
    column_ready(2)
    column(2, 0, 4)
    for ref in (kv.at[0], kv.at[1, pl.ds(0, 3)], kv.at[1, 3, pl.ds(0, 7)]):
        pltpu.make_async_copy(ref, ref, ag_send).wait()
    top = top_ref[...]
    inv = 1.0 / l_ref[...]
    out_t = acc[...] * inv
    delta = jnp.sum(out_t * dot_ref[...], axis=0, keepdims=True)
    for g in range(GROUPS):
        mo4[x, :, g * 128:(g + 1) * 128] = out_t[:, g * 128:(g + 1) * 128].T.astype(BF16)
    for t in (xr, xl, xo):
        mo_copy(x, t).start()
    states_row()
    acc[...] = jnp.zeros_like(acc)

    def sib_copy(j):
        pair = pl.ds(2 * (j % 4), 2)
        return pltpu.make_async_remote_copy(
            src_ref=dkv.at[other, j // 4, pair], dst_ref=sib.at[j // 4, pair],
            send_sem=rs_sib_send.at[j], recv_sem=rs_sib.at[j],
            device_id=p.dev(x, z, other), device_id_type=MESH)

    def sib_add(j):
        pair = pl.ds(2 * (j % 4), 2)
        sib_copy(j).wait()
        dkv[core, j // 4, pair] = add16(dkv[core, j // 4, pair], sib[j // 4, pair])

    def backward(j, c):
        factor = jnp.exp2((mst[j] - top) * (SCALE * LOG2E)) * inv
        grad = (dot_ref[...] * factor).astype(BF16)
        dw = dot(keys(j, 1), grad, 1, 0)
        w16 = pst[j]
        ds = (w16.astype(F32) * (dw - delta * factor)).astype(BF16)
        dk = dot(ds, qs[...], 1, 0) * SCALE
        dv = dot(w16, grad, 1, 1)
        acc[...] = acc[...] + dot(keys(j, 0), ds, 0, 0)
        dkv[:, j // 4, pl.ds(2 * (j % 4), 2), 0] = dk.astype(BF16).reshape(2, 2, 128, 128)
        dkv[:, j // 4, pl.ds(2 * (j % 4), 2), 1] = dv.astype(BF16).reshape(2, 2, 128, 128)
        sib_copy(j).start()
        return c

    def place(i):
        return (2 - i - i * (i - 1) // 2 + 8) % 4

    def shell(k, work):
        n = 4 - k

        def one(t, c):
            straight = t < n
            row = jnp.where(straight, k, k + 1 + t - n)
            column = jnp.where(straight, k + t, k)
            j = 4 * ((x + place(row)) % 4) + (zp + place(column)) % 4

            @pl.when(j <= diag)
            def _():
                work(j)

            return c

        lax.fori_loop(0, 2 * n - 1, one, 0)

    def backward_shell(k):
        shell(k, lambda j: backward(j, 0))

    def finish_shell(k):
        shell(k, sib_add)

    def remote(src, dst, sem, target, send=rs_send):
        return pltpu.make_async_remote_copy(
            src_ref=src, dst_ref=dst, send_sem=send, recv_sem=sem,
            device_id=target, device_id_type=MESH)

    def z_ring(mine, inbox, sems, send):
        right, left = p.dev(x, zz(1), core), p.dev(x, zz(-1), core)
        ra = remote(mine(zz(4), 0), inbox(0, 0, 0), sems.at[0, 0], right, send)
        la = remote(mine(zz(4), 1), inbox(1, 0, 1), sems.at[0, 1], left, send)
        ra.start()
        la.start()
        yield
        for s in (1, 2, 3):
            d = 4 - s
            h = 0 if s == 1 else None
            ra.wait_recv()
            ref = mine(zz(d), h)
            ref[...] = add16(ref[...], inbox(0, s - 1, h)[...])
            ra = remote(mine(zz(d)), inbox(0, s), sems.at[s, 0], right, send)
            ra.start()
            h = 1 if s == 1 else None
            la.wait_recv()
            ref = mine(zz(-d), h)
            ref[...] = add16(ref[...], inbox(1, s - 1, h)[...])
            la = remote(mine(zz(-d)), inbox(1, s), sems.at[s, 1], left, send)
            la.start()
            yield
        ra.wait_recv()
        la.wait_recv()

    def projection():
        for t in (xr, xl, xo):
            mo_copy(t, t).wait_recv()
        lg_pass(1, p.y + 2).wait_recv()
        lg_pass(3, p.y + 2).wait_recv()
        lg_turn(1).wait_send()
        lg_turn(3).wait_send()
        lg_pass(1, p.y - 1).wait_send()
        lg_pass(3, p.y + 1).wait_send()
        sent = lg4.at[pl.ds(0, 3), pl.ds(0, 32)]
        pltpu.make_async_copy(sent, sent, lg_send).wait()
        pltpu.make_async_copy(mo4.at[pl.ds(0, 3)], mo4.at[pl.ds(0, 3)], mo_send).wait()
        outs = mo4[...].reshape(512, ROWS)
        for i in range(2):
            part = dot(lg4[:, :, i * 640:(i + 1) * 640].reshape(512, 640), outs, 0, 0)
            for k in range(8):
                pj[k % 2, i * 4 + k // 2] = part[k * 80:(k + 1) * 80].astype(BF16)
        swap = remote(pj.at[other], psib, pj_sib, p.dev(x, z, other), pj_send)
        swap.start()
        yield
        swap.wait_recv()

        def one(b, c):
            pj[core, b] = add16(pj[core, b], psib[b])
            return c

        lax.fori_loop(0, 8, one, 0)

        def half_of(ref, h):
            return ref if h is None else ref.at[pl.ds(0, 48)] if h == 0 else ref.at[pl.ds(48, 32)]

        yield from z_ring(
            lambda i, h=None: half_of(pj.at[core, i], h),
            lambda way, s, h=None: half_of(pz.at[way, s], h), pj_z, pj_send)
        pg_ref[...] = pj[core, z].astype(F32) + pz[0, 3].astype(F32) + pz[1, 3].astype(F32)

    proj = projection()

    def x_half(way):
        t, target = (xo, xright) if way == 0 else (xo, xleft)
        return remote(dkv.at[0, t, :, way], x1.at[way], rs_x.at[0, way], target)

    def x_full(way):
        t, target = (xr, xright) if way == 0 else (xl, xleft)
        return remote(dkv.at[0, t], x2.at[way], rs_x.at[1, way], target)

    def z_half(way):
        return remote(dkv.at[1, :, zz(4), way], z1.at[way, 0, :, way], rs_z.at[0, way], right if way == 0 else left)

    def z_full(way, s):
        t, target = (zz(4 - s), right) if way == 0 else (zz(s - 4), left)
        return remote(dkv.at[1, :, t], z1.at[way, s], rs_z.at[s, way], target)

    def x_next(way):
        x_half(way).wait_recv()
        t = xr if way == 0 else xl
        dkv[0, t, :, way] = add16(dkv[0, t, :, way], x1[way])
        x_full(way).start()

    def z_next(way, s):
        t = zz(4 - s) if way == 0 else zz(s - 4)
        if s == 1:
            z_half(way).wait_recv()
            dkv[1, :, t, way] = add16(dkv[1, :, t, way], z1[way, 0, :, way])
        else:
            z_full(way, s - 1).wait_recv()
            dkv[1, :, t] = add16(dkv[1, :, t], z1[way, s - 1])
        z_full(way, s).start()

    def by_core(zero, one):
        pl.when(core == 0)(zero)
        pl.when(core == 1)(one)

    def both(f):
        f(0)
        f(1)

    backward_shell(0)
    finish_shell(0)
    by_core(lambda: both(lambda w: x_half(w).start()), lambda: both(lambda w: z_half(w).start()))
    states_back()
    backward_shell(1)
    next(proj, None)
    finish_shell(1)
    by_core(lambda: x_next(0), lambda: z_next(0, 1))
    backward_shell(2)
    next(proj, None)
    finish_shell(2)

    def third():
        z_next(1, 1)
        z_next(0, 2)

    by_core(lambda: x_next(1), third)
    backward_shell(3)
    states_last()
    finish_shell(3)
    for g in range(GROUPS):
        dq_ref[:, g * 128:(g + 1) * 128] = (acc[:, g * 128:(g + 1) * 128] * SCALE).T.astype(BF16)

    def sum3(a, b, c):
        return (a.astype(F32) + b.astype(F32) + c.astype(F32)).astype(BF16)

    def x_sum():
        both(lambda w: x_full(w).wait_recv())

        def one(b, c):
            dkv[0, x, b] = sum3(dkv[0, x, b], x2[0, b], x2[1, b])
            return c

        lax.fori_loop(0, 8, one, 0)
        for i in range(1, 8):
            z_in(i).start()

    def z_in(i):
        t = zz(i)
        return remote(dkv.at[0, x, t], zin.at[z], rs_zin.at[z], p.dev(x, t, 0))

    def z_sum():
        both(lambda w: z_full(w, 3).wait_recv())

        def one(b, c):
            dkv[1, b, z] = sum3(dkv[1, b, z], z1[0, 3, b], z1[1, 3, b])
            return c

        lax.fori_loop(0, 4, one, 0)
        for i in range(1, 4):
            x_in(i).start()

    def x_in(i):
        t = (x + i) % 4
        return remote(dkv.at[1, t, z], xin.at[x], rs_xin.at[x], p.dev(t, z, 1))

    def keys_out(parts):
        for ref, h in ((dk_ref, 0), (dv_ref, 1)):
            total = parts[0][h].astype(F32)
            for part in parts[1:]:
                total = total + part[h].astype(F32)
            ref[...] = total.astype(BF16)

    def last_zero():
        for i in range(1, 8):
            t = zz(i)
            remote(dkv.at[0, x, t], zin.at[t], rs_zin.at[t], p.dev(x, t, 0)).wait_recv()
        keys_out([dkv.at[0, x, z]] + [zin.at[zz(i)] for i in range(1, 8)])

    def last_one():
        for i in range(1, 4):
            t = (x + i) % 4
            remote(dkv.at[1, t, z], xin.at[t], rs_xin.at[t], p.dev(t, z, 1)).wait_recv()
        keys_out([dkv.at[1, x, z]] + [xin.at[(x + i) % 4] for i in range(1, 4)])

    def states():
        pair_copy(vx, vy, 2).wait()

        @pl.when(core == 0)
        def _():
            si[...] = in2[...].reshape(128, 1024)
            gn[...] = vy[...]

        @pl.when(core == 1)
        def _():
            gn[...] = in2[...].reshape(128, 1024)
            si[...] = vy[...]

        for g in range(2):
            narrow = slice(g * NS, (g + 1) * NS)
            wide = slice(g * HALF, (g + 1) * HALF)
            full = fed[:, wide] + tx[:, wide] * dot(w_ref[:, narrow], gn[:, wide], 1, 0)
            feed_ref[:, wide] = full.astype(BF16)
            yield
            write_ref[:, narrow] += dot(fw[:, wide], gn[:, wide], 1, 1)
            read_ref[:, narrow] += dot(gh[:, wide], si[:, wide], 1, 1)
            yield

    final = states()
    by_core(x_sum, lambda: z_next(1, 2))
    next(final)
    next(proj, None)
    by_core(lambda: None, lambda: z_next(0, 3))
    next(final)
    by_core(lambda: None, lambda: z_next(1, 3))
    next(proj, None)
    for _ in final:
        pass
    by_core(lambda: None, z_sum)
    next(proj, None)
    by_core(last_zero, last_one)
    for _ in proj:
        pass

    for ref in (kv.at[0, pl.ds(0, 3)], kv.at[0, 3, pl.ds(0, 7)]):
        pltpu.make_async_copy(ref, ref, rs_send).wait()
    for ref in (pj.at[0], pj.at[1, pl.ds(0, 7)]):
        pltpu.make_async_copy(ref, ref, pj_send).wait()


def copy_kernel(*refs):
    for i in range(7):
        refs[7 + i][...] = refs[i][...]


def per_device(query_rows, key_rows, value_rows, mixed_grad, layer_grad,
               state_feed, write_map, read_map, log_decay, scan_grad):
    vm = pl.BlockSpec(memory_space=pltpu.VMEM)
    dma = pltpu.SemaphoreType.DMA

    def out(shape, dtype):
        return jax.ShapeDtypeStruct(shape, dtype)

    shapes = (
            out((128, ROWS), BF16),
            out((128, 128), BF16),
            out((128, 128), BF16),
            out((80, ROWS), F32),
            out((128, 1024), BF16),
            out((128, 256), F32),
            out((128, 256), F32),
    )
    results = pl.pallas_call(
        kernel,
        out_shape=shapes,
        in_specs=[vm] * 4 + [pl.BlockSpec(memory_space=pl.ANY)] + [vm] * 5,
        out_specs=(vm,) * 7,
        scratch_shapes=[
            pltpu.VMEM((2, 4, 8, 2, 128, 128), BF16),
            pltpu.VMEM((2, 4, 8, 2, 128, 128), BF16),
            pltpu.VMEM((16, TK, ROWS), BF16),
            pltpu.VMEM((ROWS, HD), BF16),
            pltpu.VMEM((HD, ROWS), F32),
            pltpu.VMEM((16, 1, ROWS), F32),
            pltpu.VMEM((1, ROWS), F32),
            pltpu.VMEM((1, ROWS), F32),
            pltpu.VMEM((HD, ROWS), F32),
            pltpu.VMEM((4, 8, 2, 128, 128), BF16),
            pltpu.VMEM((2, 8, 128, 128), BF16),
            pltpu.VMEM((2, 8, 2, 128, 128), BF16),
            pltpu.VMEM((2, 4, 4, 2, 128, 128), BF16),
            pltpu.VMEM((4, 2, 128, 128), BF16),
            pltpu.VMEM((8, 2, 128, 128), BF16),
            pltpu.VMEM((4, 128, ROWS), BF16),
            pltpu.VMEM((4, 128, COLS), BF16),
            pltpu.VMEM((2, 8, 80, ROWS), BF16),
            pltpu.VMEM((8, 80, ROWS), BF16),
            pltpu.VMEM((2, 4, 80, ROWS), BF16),
            pltpu.VMEM((128, 128), F32),
            pltpu.VMEM((128, 128), F32),
            pltpu.VMEM((128, 128), F32),
            pltpu.VMEM((128, 1024), F32),
            pltpu.VMEM((128, 1024), BF16),
            pltpu.VMEM((128, 1024), BF16),
            pltpu.VMEM((128, 1024), F32),
            pltpu.VMEM((128, 128), F32),
            pltpu.VMEM((128, 1024), F32),
            pltpu.VMEM((128, 1024), BF16),
            pltpu.VMEM((128, 1024), BF16),
            pltpu.VMEM((8, 1024), F32),
            pltpu.VMEM((8, 1024), F32),
            pltpu.VMEM((8, 16, 1024), BF16),
            pltpu.VMEM((8, 8, 1024), F32),
            pltpu.VMEM((8, 16, 1024), BF16),
            pltpu.VMEM((4, 24, 1024), F32),
            pltpu.VMEM((8, 16, 1024), BF16),
            pltpu.VMEM((8, 16, 1024), BF16),
            pltpu.VMEM((128, 1024), BF16),
            pltpu.VMEM((128, 1024), BF16),
            pltpu.VMEM((128, 1024), BF16),
            pltpu.VMEM((128, 1024), BF16),
            dma, dma((4, 8, 2)), dma((4, 8)),
            dma, dma((16,)), dma((16,)), dma((2, 2)), dma((4, 2)), dma((4,)), dma((8,)),
            dma, dma((4,)), dma, dma((4,)), dma, dma((2, 4)), dma, dma, dma((4, 2)),
            dma((3, 2)), dma((2, 2, 8)), dma((2, 4)), dma((2, 8)), dma,
        ],
        compiler_params=pltpu.CompilerParams(
            collective_id=0, has_side_effects=True, vmem_limit_bytes=58 * 2**20
        ),
    )(query_rows, key_rows, value_rows, mixed_grad, layer_grad,
      state_feed, write_map, read_map, log_decay.T, scan_grad)
    return pl.pallas_call(
        copy_kernel,
        out_shape=shapes,
        in_specs=[vm] * 7,
        out_specs=(vm,) * 7,
    )(*results)


def solution(mesh):
    split = P("ctx", "fsdp")
    return jax.shard_map(
        per_device,
        mesh=mesh,
        in_specs=(split,) * 4 + (P("ctx", None),) + (split,) * 5,
        out_specs=(split,) * 7,
        check_vma=False,
    )
```

```python
import functools
import jax
import jax.numpy as jnp
from jax import lax
from jax.experimental import pallas as pl
from jax.experimental.pallas import tpu as pltpu
from jax.sharding import PartitionSpec as P

HD = 128
NS = 128
HALF = 512
COLS = 1280
GROUPS = 5
ROWS = 128 * GROUPS
TK = 512
SCALE = HD ** (-0.5)
LOG2E = 1.4426950408889634
MESH = pl.DeviceIdType.MESH
F32 = jnp.float32
BF16 = jnp.bfloat16


def dot(a, b, ca, cb):
    return lax.dot_general(a, b, (((ca,), (cb,)), ((), ())), preferred_element_type=F32)


class Place:
    def __init__(self):
        self.me = lax.axis_index("ctx")
        self.y = lax.axis_index("fsdp")
        self.core = self.me % 2
        self.z = (self.me // 2) % 8
        self.x = self.me // 16

    def dev(self, x, z, core):
        return ((x * 8 + z) * 2 + core, self.y)

    def across(self, step):
        return (self.me, (self.y + step) % 4)


def exact(a, b):
    return lax.dot_general(
        a, b, (((1,), (0,)), ((), ())), preferred_element_type=F32, precision=lax.Precision.HIGHEST
    )


def add16(a, b):
    return a + b


def in_turns(order, *steps):
    for i in order:
        next(steps[i], None)
    for step in steps:
        for _ in step:
            pass


def kernel(q_ref, k_ref, v_ref, do_ref, lg_ref, f_ref, w_ref, r_ref, ld_ref, g_ref,
           dq_ref, dk_ref, dv_ref, pg_ref, feed_ref, write_ref, read_ref,
           kv, dkv, pst, qs, dot_ref, mst, l_ref, top_ref, acc, sib,
           x1, x2, z1, xin, zin,
           mo4, lg4, pj, psib, pz,
           lds, a_ref, at_ref, tx, fw, gh, fed, inner,
           mine_s, sx, sy, lt, ls, t16, cdl, in1, xt, out2, in2, vx, vy, si, gn,
           ag_send, ag_recv, sib_recv, rs_send, rs_sib_send, rs_sib, rs_x, rs_z, rs_xin, rs_zin,
           mo_send, mo_recv, lg_send, lg_recv, lg_own, lg_y, pj_send, pj_sib, pj_z,
           s_pair, s_z, s_x, s_back, s_last):
    p = Place()
    me, x, z, core = p.me, p.x, p.z, p.core
    other = 1 - core

    barrier = pltpu.get_barrier_semaphore()

    def zz(s):
        return (z + s + 8) % 8

    xr, xl, xo = (x + 1) % 4, (x + 3) % 4, (x + 2) % 4
    partners = [p.dev(x, z, other)] + [p.dev(t, z, core) for t in (xr, xl, xo)]
    partners += [p.dev(x, zz(i), core) for i in range(1, 8)]
    partners += [p.across(1), p.across(3)]
    for t in partners:
        pl.semaphore_signal(barrier, inc=1, device_id=t, device_id_type=MESH)
    kv[core, x, z, 0] = k_ref[...]
    kv[core, x, z, 1] = v_ref[...]
    pl.semaphore_wait(barrier, 13)

    def push(c, bx, bz, half, target):
        if half is None:
            src, sem = kv.at[c, bx, bz], ag_recv.at[bx, bz, 0]
        else:
            src, sem = kv.at[c, bx, bz, half], ag_recv.at[bx, bz, half]
        pltpu.make_async_remote_copy(
            src_ref=src, dst_ref=src, send_sem=ag_send, recv_sem=sem,
            device_id=target, device_id_type=MESH).start()

    def sibling(c, bx, bz):
        pltpu.make_async_remote_copy(
            src_ref=kv.at[c, bx, bz], dst_ref=kv.at[c, bx, bz], send_sem=ag_send,
            recv_sem=sib_recv.at[bx, bz], device_id=p.dev(x, z, 1 - c), device_id_type=MESH).start()

    def got(c, bx, bz, half=None):
        if half is None:
            ref, sem = kv.at[c, bx, bz], ag_recv.at[bx, bz, 0]
        else:
            ref, sem = kv.at[c, bx, bz, half], ag_recv.at[bx, bz, half]
        pltpu.make_async_remote_copy(
            src_ref=ref, dst_ref=ref, send_sem=ag_send, recv_sem=sem,
            device_id=p.dev(x, z, 1 - c), device_id_type=MESH).wait_recv()

    @pl.when(core == 0)
    def _():
        push(0, x, z, None, p.dev(x, zz(1), 0))
        push(0, x, z, None, p.dev(x, zz(-1), 0))
        push(0, x, z, None, p.dev(xr, z, 0))
        push(0, x, z, None, p.dev(xl, z, 0))
        sibling(0, x, z)

    @pl.when(core == 1)
    def _():
        push(1, x, z, None, p.dev(xr, z, 1))
        push(1, x, z, None, p.dev(xl, z, 1))
        push(1, x, z, None, p.dev(xo, z, 1))
        push(1, x, z, None, p.dev(x, zz(1), 1))
        push(1, x, z, None, p.dev(x, zz(-1), 1))
        sibling(1, x, z)

    for g in range(GROUPS):
        cols = pl.ds(g * 128, 128)
        qs[g * 128:(g + 1) * 128, :] = q_ref[:, cols]
        dot_ref[:, cols] = do_ref[:, cols].astype(F32).T

    def zero(i, c):
        dkv[i // 32, (i // 8) % 4, i % 8] = jnp.zeros((2, 128, 128), BF16)
        return c

    lax.fori_loop(0, 64, zero, 0)
    acc[...] = jnp.zeros_like(acc)
    l_ref[...] = jnp.zeros_like(l_ref)
    top_ref[...] = jnp.full_like(top_ref, -1e30)

    def pair_copy(src, dst, i):
        return pltpu.make_async_remote_copy(
            src_ref=src, dst_ref=dst, send_sem=s_pair.at[i, 0], recv_sem=s_pair.at[i, 1],
            device_id=p.dev(x, z, other), device_id_type=MESH)

    def states_alone():
        row = lax.broadcasted_iota(jnp.int32, (128, 128), 0)
        col = lax.broadcasted_iota(jnp.int32, (128, 128), 1)
        lds[...] = jnp.zeros_like(lds)
        lds[0:16, :] = ld_ref[...]
        running = exact((row >= col).astype(F32), lds[...].T)
        a_ref[...] = running
        at_ref[...] = running.T
        total = running[127:128, :]
        spread_heads = (
            lax.broadcasted_iota(jnp.int32, (128, 1024), 1) // 64
            == lax.broadcasted_iota(jnp.int32, (128, 1024), 0)
        ).astype(F32)
        tx[...] = exact(jnp.exp(total - running), spread_heads)
        fw[...] = (f_ref[...].astype(F32) * tx[...]).astype(BF16)
        gh[...] = (g_ref[...].astype(F32) * exact(jnp.exp(running), spread_heads)).astype(BF16)
        lt[...] = exact(jnp.broadcast_to(total, (8, 128)), spread_heads)
        for g in range(2):
            wide = slice(g * HALF, (g + 1) * HALF)
            narrow = slice(g * NS, (g + 1) * NS)
            state = dot(w_ref[:, narrow], fw[:, wide], 0, 0)
            back = dot(r_ref[:, narrow], gh[:, wide], 0, 0)

            @pl.when(core == 0)
            def _():
                mine_s[:, wide] = state
                sx[:, wide] = back.astype(BF16)

            @pl.when(core == 1)
            def _():
                mine_s[:, wide] = back
                sx[:, wide] = state.astype(BF16)

        pair_copy(sx, sy, 0).start()
        pair_copy(lt, ls, 1).start()
        yield
        low_half = col < 64

        def two(value):
            full = value.astype(F32)
            return jnp.concatenate(
                [jnp.where(low_half, full, 0.0), jnp.where(low_half, 0.0, full)], axis=0
            ).astype(BF16)

        for g in range(2):
            narrow = slice(g * NS, (g + 1) * NS)
            pairing = dot(w_ref[:, narrow], r_ref[:, narrow], 1, 1)
            inner[...] = jnp.zeros_like(inner)
            for k in range(4):
                lanes = slice(g * HALF + k * 128, g * HALF + (k + 1) * 128)
                head = g * 8 + 2 * k
                decays = []
                for h in (head, head + 1):
                    gap = at_ref[h:h + 1, :] - a_ref[:, h:h + 1]
                    decays.append(jnp.where(col >= row, jnp.exp(jnp.where(col >= row, gap, 0.0)), 0.0))
                grads = g_ref[:, lanes]
                cross = dot(two(f_ref[:, lanes]), grads, 1, 1)
                inner[...] += decays[0] * cross[0:128] + decays[1] * cross[128:256]
                mixed = jnp.concatenate([d * pairing for d in decays], axis=1).astype(BF16)
                fed[:, lanes] = dot(mixed, two(grads), 1, 0)
                yield
            inner16 = inner[...].astype(BF16)
            write_ref[:, narrow] = dot(inner16, r_ref[:, narrow], 1, 0)
            read_ref[:, narrow] = dot(inner16, w_ref[:, narrow], 0, 0)

    right, left = p.dev(x, zz(1), core), p.dev(x, zz(-1), core)
    xright, xleft = p.dev(xr, z, core), p.dev(xl, z, core)

    def spread_x(bz):
        push(0, x, bz, None, xright)
        push(0, x, bz, None, xleft)
        sibling(0, x, bz)

    def across(bz):
        got(0, xl, bz)
        push(0, xl, bz, 0, xright)
        sibling(0, xl, bz)
        got(0, xr, bz)
        push(0, xr, bz, 1, xleft)
        sibling(0, xr, bz)

    def opposite(bz):
        got(0, xo, bz, 0)
        got(0, xo, bz, 1)
        sibling(0, xo, bz)

    def row_step(s):
        got(0, x, zz(-s))
        push(0, x, zz(-s), None if s < 3 else 0, right)
        spread_x(zz(-s))
        got(0, x, zz(s))
        push(0, x, zz(s), None if s < 3 else 1, left)
        spread_x(zz(s))

    def spread_z(bx):
        push(1, bx, z, None, right)
        push(1, bx, z, None, left)
        sibling(1, bx, z)

    def along(bx, s):
        got(1, bx, zz(-s))
        push(1, bx, zz(-s), None if s < 3 else 0, right)
        sibling(1, bx, zz(-s))
        got(1, bx, zz(s))
        push(1, bx, zz(s), None if s < 3 else 1, left)
        sibling(1, bx, zz(s))

    def first(k):
        if k == 0:
            row_step(1)
        elif k == 1:
            across(z)
            row_step(2)
        elif k == 2:
            across(zz(-1))
            across(zz(1))
            opposite(z)
            row_step(3)
        elif k == 3:
            opposite(zz(-1))
            opposite(zz(1))
            across(zz(-2))
            across(zz(2))
            got(0, x, zz(4), 0)
            got(0, x, zz(4), 1)
            spread_x(zz(4))
        elif k == 4:
            across(zz(-3))
            across(zz(3))
            opposite(zz(-2))
            opposite(zz(2))
        elif k == 5:
            across(zz(4))
            opposite(zz(-3))
            opposite(zz(3))
        else:
            opposite(zz(4))

    def second(k):
        if k == 0:
            got(1, xl, z)
            spread_z(xl)
            got(1, xr, z)
            spread_z(xr)
            along(x, 1)
            got(1, xo, z)
            spread_z(xo)
        elif k == 1:
            along(xl, 1)
            along(xr, 1)
        elif k == 2:
            along(x, 2)
            along(xo, 1)
        elif k == 3:
            along(xl, 2)
            along(xr, 2)
            along(x, 3)
            along(xo, 2)
        elif k == 4:
            along(xl, 3)
            along(xr, 3)
            along(xo, 3)
        elif k == 5:
            for bx in (x, xl):
                got(1, bx, zz(4), 0)
                got(1, bx, zz(4), 1)
                sibling(1, bx, zz(4))
        else:
            for bx in (xr, xo):
                got(1, bx, zz(4), 0)
                got(1, bx, zz(4), 1)
                sibling(1, bx, zz(4))

    def gather(k):
        @pl.when(core == 0)
        def _():
            first(k)

        @pl.when(core == 1)
        def _():
            second(k)

    def order(k, n):
        return k + core * (n - 1 - 2 * k)

    def z_copy(i, src, dst, sems, slot):
        t = zz(i)
        return pltpu.make_async_remote_copy(
            src_ref=src.at[slot(t)], dst_ref=dst.at[z], send_sem=sems.at[0, i], recv_sem=sems.at[1, z],
            device_id=p.dev(x, t, core), device_id_type=MESH)

    def z_wait(i, src, dst, sems, slot):
        t = zz(i)
        pltpu.make_async_remote_copy(
            src_ref=src.at[slot(t)], dst_ref=dst.at[t], send_sem=sems.at[0, i], recv_sem=sems.at[1, t],
            device_id=p.dev(x, t, core), device_id_type=MESH).wait()

    def at_target(t):
        return t

    def at_home(t):
        return z

    def states_join():
        pair_copy(sx, sy, 0).wait()
        pair_copy(lt, ls, 1).wait()
        joined = jnp.exp(ls[0:1, :]) * mine_s[...] + sy[...].astype(F32)
        t16[...] = joined.astype(BF16).reshape(8, 16, 1024)
        cdl[z] = lt[...] + ls[...]
        for i in range(1, 8):
            z_copy(i, t16, in1, s_z.at[0], at_target).start()
            z_copy(i, cdl, cdl, s_z.at[1], at_home).start()
        in1[z] = t16[z]

    def x_copy(i, t):
        return pltpu.make_async_remote_copy(
            src_ref=xt.at[i], dst_ref=xt.at[i], send_sem=s_x.at[0, (t - x + 4) % 4], recv_sem=s_x.at[1, i],
            device_id=p.dev(t, z, core), device_id_type=MESH)

    def along_row(state, keep):
        for k in range(8):
            c = order(k, 8)
            if keep:
                out2[c] = state.astype(BF16)
            state = jnp.exp(cdl[c, 0:1, :]) * state + in1[c].astype(F32)
        return state

    def states_row():
        for i in range(1, 8):
            z_wait(i, t16, in1, s_z.at[0], at_target)
            z_wait(i, cdl, cdl, s_z.at[1], at_home)
        xt[x, 0:16, :] = along_row(jnp.zeros((16, 1024), F32), False)
        summed = cdl[0]
        for k in range(1, 8):
            summed = summed + cdl[k]
        xt[x, 16:24, :] = summed
        for t in (xr, xl, xo):
            x_copy(x, t).start()

    def states_back():
        for t in (xr, xl, xo):
            x_copy(x, t).wait_send()
            x_copy(t, t).wait_recv()
        state = jnp.zeros((16, 1024), F32)
        mine_at = order(0, 4) + x - 2 * core * x
        for k in range(3):
            c = order(k, 4)
            later = jnp.exp(xt[c, 16:17, :]) * state + xt[c, 0:16, :]
            state = jnp.where(k < mine_at, later, state)
        along_row(state, True)
        for i in range(1, 8):
            z_copy(i, out2, in2, s_back, at_target).start()
        in2[z] = out2[z]

    def states_last():
        for i in range(1, 8):
            z_wait(i, out2, in2, s_back, at_target)
        entered = in2[...].reshape(128, 1024)
        vx[...] = (jnp.exp(lt[0:1, :]) * entered.astype(F32) + mine_s[...]).astype(BF16)
        pair_copy(vx, vy, 2).start()

    def columns(i):
        return pl.ds(pl.multiple_of(i * COLS, 128), COLS)

    def quarter(y):
        return pl.ds(pl.multiple_of(((y + 4) % 4) * 32, 32), 32)

    def lg_copy(i, t):
        return pltpu.make_async_remote_copy(
            src_ref=lg_ref.at[quarter(p.y), columns(t)], dst_ref=lg4.at[i, quarter(p.y)],
            send_sem=lg_send, recv_sem=lg_recv.at[i],
            device_id=p.dev(t, z, core), device_id_type=MESH)

    def lg_turn(step):
        ref = lg4.at[:, quarter(p.y)]
        return pltpu.make_async_remote_copy(
            src_ref=ref, dst_ref=ref, send_sem=lg_y.at[0, step // 2], recv_sem=lg_y.at[1, step // 2],
            device_id=p.across(step), device_id_type=MESH)

    def lg_from(step):
        ref = lg4.at[:, quarter(p.y + step)]
        return pltpu.make_async_remote_copy(
            src_ref=ref, dst_ref=ref, send_sem=lg_y.at[0, 0], recv_sem=lg_y.at[1, 1 - step // 2],
            device_id=p.across(step), device_id_type=MESH)

    def lg_pass(step, y):
        ref = lg4.at[pl.ds(step - 1, 2), quarter(y)]
        return pltpu.make_async_remote_copy(
            src_ref=ref, dst_ref=ref, send_sem=lg_y.at[0, 2 + step // 2], recv_sem=lg_y.at[1, 2 + step // 2],
            device_id=p.across(step), device_id_type=MESH)

    def mo_copy(i, t):
        return pltpu.make_async_remote_copy(
            src_ref=mo4.at[i], dst_ref=mo4.at[i], send_sem=mo_send, recv_sem=mo_recv.at[i],
            device_id=p.dev(t, z, core), device_id_type=MESH)

    lg_mine = pltpu.make_async_copy(
        lg_ref.at[quarter(p.y), columns(x)], lg4.at[x, quarter(p.y)], lg_own)
    lg_mine.start()
    for t in (xr, xl, xo):
        lg_copy(x, t).start()

    diag = me // 4
    zp = z // 2

    def keys(j, which):
        return kv[:, j // 4, pl.ds(2 * (j % 4), 2), which].reshape(TK, HD)

    def forward(j, masked):
        top = top_ref[...]
        s = dot(keys(j, 0), qs[...], 1, 1)
        if masked:
            r = lax.broadcasted_iota(jnp.int32, (TK, ROWS), 0)
            c = lax.broadcasted_iota(jnp.int32, (TK, ROWS), 1)
            pos = ((j * 4 + ((r // 128) % 2) * 2 + r // 256) * 128) + r % 128
            s = jnp.where(pos <= me * 128 + c % 128, s, -1e30)
        new = jnp.maximum(top, jnp.max(s, axis=0, keepdims=True))
        w = jnp.exp2((s - new) * (SCALE * LOG2E))
        shrink = jnp.exp2((top - new) * (SCALE * LOG2E))
        l_ref[...] = l_ref[...] * shrink + jnp.sum(w, axis=0, keepdims=True)
        w16 = w.astype(BF16)
        pst[j] = w16
        mst[j] = new
        top_ref[...] = new
        acc[...] = acc[...] * shrink + dot(keys(j, 1), w16, 0, 0)

    def sib_wait(bx, bz):
        pltpu.make_async_remote_copy(
            src_ref=kv.at[other, bx, bz], dst_ref=kv.at[other, bx, bz], send_sem=ag_send,
            recv_sem=sib_recv.at[bx, bz], device_id=p.dev(x, z, other), device_id_type=MESH).wait_recv()

    def column_ready(i):
        c = (zp + i) % 4

        def one(b, carry):
            sib_wait(b // 2, 2 * c + b % 2)
            return carry

        lax.fori_loop(0, 8, one, 0)

    def column(i, start, stop):
        c = (zp + i) % 4

        def one(b, carry):
            forward(4 * b + c, False)
            return carry

        lax.fori_loop(start, jnp.minimum(stop, (diag - c + 3) // 4), one, 0)

    alone = states_alone()
    next(alone)
    gather(0)
    next(alone)
    next(alone)
    gather(1)
    next(alone)
    next(alone)
    gather(2)
    next(alone)
    next(alone)
    gather(3)
    for _ in alone:
        pass
    lg_mine.wait()
    for t in (xr, xl, xo):
        lg_copy(t, t).wait_recv()
    lg_turn(1).start()
    lg_turn(3).start()
    column_ready(0)
    forward(diag, True)
    gather(4)
    column(0, 0, 4)
    states_join()
    gather(5)
    column_ready(1)
    column_ready(3)
    column(1, 0, 4)
    gather(6)
    for step in (1, 3):
        lg_from(step).wait_recv()
    lg_pass(1, p.y - 1).start()
    lg_pass(3, p.y + 1).start()
    column(3, 0, 4)
    states_row()
    column_ready(2)
    column(2, 0, 4)
    for ref in (kv.at[0], kv.at[1, pl.ds(0, 3)], kv.at[1, 3, pl.ds(0, 7)]):
        pltpu.make_async_copy(ref, ref, ag_send).wait()
    top = top_ref[...]
    inv = 1.0 / l_ref[...]
    out_t = acc[...] * inv
    delta = jnp.sum(out_t * dot_ref[...], axis=0, keepdims=True)
    for g in range(GROUPS):
        mo4[x, :, g * 128:(g + 1) * 128] = out_t[:, g * 128:(g + 1) * 128].T.astype(BF16)
    for t in (xr, xl, xo):
        mo_copy(x, t).start()
    acc[...] = jnp.zeros_like(acc)

    def sib_copy(j):
        pair = pl.ds(2 * (j % 4), 2)
        return pltpu.make_async_remote_copy(
            src_ref=dkv.at[other, j // 4, pair], dst_ref=sib.at[j // 4, pair],
            send_sem=rs_sib_send.at[j], recv_sem=rs_sib.at[j],
            device_id=p.dev(x, z, other), device_id_type=MESH)

    def sib_add(j):
        pair = pl.ds(2 * (j % 4), 2)
        sib_copy(j).wait()
        dkv[core, j // 4, pair] = add16(dkv[core, j // 4, pair], sib[j // 4, pair])

    def backward(j, c):
        factor = jnp.exp2((mst[j] - top) * (SCALE * LOG2E)) * inv
        grad = (dot_ref[...] * factor).astype(BF16)
        dw = dot(keys(j, 1), grad, 1, 0)
        w16 = pst[j]
        ds = (w16.astype(F32) * (dw - delta * factor)).astype(BF16)
        dk = dot(ds, qs[...], 1, 0) * SCALE
        dv = dot(w16, grad, 1, 1)
        acc[...] = acc[...] + dot(keys(j, 0), ds, 0, 0)
        dkv[:, j // 4, pl.ds(2 * (j % 4), 2), 0] = dk.astype(BF16).reshape(2, 2, 128, 128)
        dkv[:, j // 4, pl.ds(2 * (j % 4), 2), 1] = dv.astype(BF16).reshape(2, 2, 128, 128)
        sib_copy(j).start()
        return c

    def place(i):
        return (2 - i - i * (i - 1) // 2 + 8) % 4

    def shell(k, whole_column, work):
        def one(t, c):
            row, column = (t, k) if whole_column else (k, t)
            j = 4 * ((x + place(row)) % 4) + (zp + place(column)) % 4

            @pl.when(j <= diag)
            def _():
                work(j)

            return c

        lax.fori_loop(k if whole_column else k + 1, 4, one, 0)

    def backward_shell(k, whole_column):
        shell(k, whole_column, lambda j: backward(j, 0))

    def finish_shell(k, whole_column):
        shell(k, whole_column, sib_add)

    def remote(src, dst, sem, target, send=rs_send):
        return pltpu.make_async_remote_copy(
            src_ref=src, dst_ref=dst, send_sem=send, recv_sem=sem,
            device_id=target, device_id_type=MESH)

    def z_ring(mine, inbox, sems, send):
        right, left = p.dev(x, zz(1), core), p.dev(x, zz(-1), core)
        ra = remote(mine(zz(4), 0), inbox(0, 0, 0), sems.at[0, 0], right, send)
        la = remote(mine(zz(4), 1), inbox(1, 0, 1), sems.at[0, 1], left, send)
        ra.start()
        la.start()
        yield
        for s in (1, 2, 3):
            d = 4 - s
            h = 0 if s == 1 else None
            ra.wait_recv()
            ref = mine(zz(d), h)
            ref[...] = add16(ref[...], inbox(0, s - 1, h)[...])
            ra = remote(mine(zz(d)), inbox(0, s), sems.at[s, 0], right, send)
            ra.start()
            h = 1 if s == 1 else None
            la.wait_recv()
            ref = mine(zz(-d), h)
            ref[...] = add16(ref[...], inbox(1, s - 1, h)[...])
            la = remote(mine(zz(-d)), inbox(1, s), sems.at[s, 1], left, send)
            la.start()
            yield
        ra.wait_recv()
        la.wait_recv()

    def projection():
        for t in (xr, xl, xo):
            mo_copy(t, t).wait_recv()
        lg_pass(1, p.y + 2).wait_recv()
        lg_pass(3, p.y + 2).wait_recv()
        lg_turn(1).wait_send()
        lg_turn(3).wait_send()
        lg_pass(1, p.y - 1).wait_send()
        lg_pass(3, p.y + 1).wait_send()
        sent = lg4.at[pl.ds(0, 3), pl.ds(0, 32)]
        pltpu.make_async_copy(sent, sent, lg_send).wait()
        pltpu.make_async_copy(mo4.at[pl.ds(0, 3)], mo4.at[pl.ds(0, 3)], mo_send).wait()
        outs = mo4[...].reshape(512, ROWS)
        for i in range(2):
            part = dot(lg4[:, :, i * 640:(i + 1) * 640].reshape(512, 640), outs, 0, 0)
            for k in range(8):
                pj[k % 2, i * 4 + k // 2] = part[k * 80:(k + 1) * 80].astype(BF16)
        swap = remote(pj.at[other], psib, pj_sib, p.dev(x, z, other), pj_send)
        swap.start()
        yield
        swap.wait_recv()

        def one(b, c):
            pj[core, b] = add16(pj[core, b], psib[b])
            return c

        lax.fori_loop(0, 8, one, 0)

        def half_of(ref, h):
            return ref if h is None else ref.at[pl.ds(0, 48)] if h == 0 else ref.at[pl.ds(48, 32)]

        yield from z_ring(
            lambda i, h=None: half_of(pj.at[core, i], h),
            lambda way, s, h=None: half_of(pz.at[way, s], h), pj_z, pj_send)
        pg_ref[...] = pj[core, z].astype(F32) + pz[0, 3].astype(F32) + pz[1, 3].astype(F32)

    proj = projection()

    def x_half(way):
        t, target = (xo, xright) if way == 0 else (xo, xleft)
        return remote(dkv.at[0, t, :, way], x1.at[way], rs_x.at[0, way], target)

    def x_full(way):
        t, target = (xr, xright) if way == 0 else (xl, xleft)
        return remote(dkv.at[0, t], x2.at[way], rs_x.at[1, way], target)

    def z_half(way):
        return remote(dkv.at[1, :, zz(4), way], z1.at[way, 0, :, way], rs_z.at[0, way], right if way == 0 else left)

    def z_full(way, s):
        t, target = (zz(4 - s), right) if way == 0 else (zz(s - 4), left)
        return remote(dkv.at[1, :, t], z1.at[way, s], rs_z.at[s, way], target)

    def x_next(way):
        x_half(way).wait_recv()
        t = xr if way == 0 else xl
        dkv[0, t, :, way] = add16(dkv[0, t, :, way], x1[way])
        x_full(way).start()

    def z_next(way, s):
        t = zz(4 - s) if way == 0 else zz(s - 4)
        if s == 1:
            z_half(way).wait_recv()
            dkv[1, :, t, way] = add16(dkv[1, :, t, way], z1[way, 0, :, way])
        else:
            z_full(way, s - 1).wait_recv()
            dkv[1, :, t] = add16(dkv[1, :, t], z1[way, s - 1])
        z_full(way, s).start()

    def by_core(zero, one):
        pl.when(core == 0)(zero)
        pl.when(core == 1)(one)

    def both(f):
        f(0)
        f(1)

    def nothing():
        pass

    backward_shell(0, True)
    states_back()
    finish_shell(0, True)
    by_core(nothing, lambda: both(lambda w: z_half(w).start()))
    backward_shell(0, False)
    finish_shell(0, False)
    by_core(lambda: both(lambda w: x_half(w).start()), nothing)
    next(proj, None)
    backward_shell(1, True)
    next(proj, None)
    finish_shell(1, True)
    by_core(nothing, lambda: z_next(0, 1))
    backward_shell(1, False)
    backward_shell(2, True)
    finish_shell(1, False)
    finish_shell(2, True)
    by_core(lambda: x_next(0), lambda: z_next(1, 1))
    next(proj, None)
    backward_shell(2, False)
    backward_shell(3, True)
    finish_shell(2, False)
    by_core(lambda: x_next(1), lambda: z_next(0, 2))
    states_last()
    finish_shell(3, True)
    for g in range(GROUPS):
        dq_ref[:, g * 128:(g + 1) * 128] = (acc[:, g * 128:(g + 1) * 128] * SCALE).T.astype(BF16)

    def sum3(a, b, c):
        return (a.astype(F32) + b.astype(F32) + c.astype(F32)).astype(BF16)

    def x_sum():
        both(lambda w: x_full(w).wait_recv())

        def one(b, c):
            dkv[0, x, b] = sum3(dkv[0, x, b], x2[0, b], x2[1, b])
            return c

        lax.fori_loop(0, 8, one, 0)
        for i in range(1, 8):
            z_in(i).start()

    def z_in(i):
        t = zz(i)
        return remote(dkv.at[0, x, t], zin.at[z], rs_zin.at[z], p.dev(x, t, 0))

    def z_sum():
        both(lambda w: z_full(w, 3).wait_recv())

        def one(b, c):
            dkv[1, b, z] = sum3(dkv[1, b, z], z1[0, 3, b], z1[1, 3, b])
            return c

        lax.fori_loop(0, 4, one, 0)
        for i in range(1, 4):
            x_in(i).start()

    def x_in(i):
        t = (x + i) % 4
        return remote(dkv.at[1, t, z], xin.at[x], rs_xin.at[x], p.dev(t, z, 1))

    def keys_out(parts):
        for ref, h in ((dk_ref, 0), (dv_ref, 1)):
            total = parts[0][h].astype(F32)
            for part in parts[1:]:
                total = total + part[h].astype(F32)
            ref[...] = total.astype(BF16)

    def last_zero():
        for i in range(1, 8):
            t = zz(i)
            remote(dkv.at[0, x, t], zin.at[t], rs_zin.at[t], p.dev(x, t, 0)).wait_recv()
        keys_out([dkv.at[0, x, z]] + [zin.at[zz(i)] for i in range(1, 8)])

    def last_one():
        for i in range(1, 4):
            t = (x + i) % 4
            remote(dkv.at[1, t, z], xin.at[t], rs_xin.at[t], p.dev(t, z, 1)).wait_recv()
        keys_out([dkv.at[1, x, z]] + [xin.at[(x + i) % 4] for i in range(1, 4)])

    def states():
        pair_copy(vx, vy, 2).wait()

        @pl.when(core == 0)
        def _():
            si[...] = in2[...].reshape(128, 1024)
            gn[...] = vy[...]

        @pl.when(core == 1)
        def _():
            gn[...] = in2[...].reshape(128, 1024)
            si[...] = vy[...]

        for g in range(2):
            narrow = slice(g * NS, (g + 1) * NS)
            wide = slice(g * HALF, (g + 1) * HALF)
            full = fed[:, wide] + tx[:, wide] * dot(w_ref[:, narrow], gn[:, wide], 1, 0)
            feed_ref[:, wide] = full.astype(BF16)
            yield
            write_ref[:, narrow] += dot(fw[:, wide], gn[:, wide], 1, 1)
            read_ref[:, narrow] += dot(gh[:, wide], si[:, wide], 1, 1)
            yield

    final = states()
    by_core(nothing, lambda: z_next(1, 2))
    next(proj, None)
    by_core(x_sum, lambda: z_next(0, 3))
    next(final)
    by_core(nothing, lambda: z_next(1, 3))
    next(proj, None)
    for _ in final:
        pass
    by_core(nothing, z_sum)
    for _ in proj:
        pass
    by_core(last_zero, last_one)
    for ref in (kv.at[0, pl.ds(0, 3)], kv.at[0, 3, pl.ds(0, 7)]):
        pltpu.make_async_copy(ref, ref, rs_send).wait()
    for ref in (pj.at[0], pj.at[1, pl.ds(0, 7)]):
        pltpu.make_async_copy(ref, ref, pj_send).wait()


def copy_kernel(*refs):
    for i in range(7):
        refs[7 + i][...] = refs[i][...]


def per_device(query_rows, key_rows, value_rows, mixed_grad, layer_grad,
               state_feed, write_map, read_map, log_decay, scan_grad):
    vm = pl.BlockSpec(memory_space=pltpu.VMEM)
    dma = pltpu.SemaphoreType.DMA

    def out(shape, dtype):
        return jax.ShapeDtypeStruct(shape, dtype)

    shapes = (
            out((128, ROWS), BF16),
            out((128, 128), BF16),
            out((128, 128), BF16),
            out((80, ROWS), F32),
            out((128, 1024), BF16),
            out((128, 256), F32),
            out((128, 256), F32),
    )
    results = pl.pallas_call(
        kernel,
        out_shape=shapes,
        in_specs=[vm] * 4 + [pl.BlockSpec(memory_space=pl.ANY)] + [vm] * 5,
        out_specs=(vm,) * 7,
        scratch_shapes=[
            pltpu.VMEM((2, 4, 8, 2, 128, 128), BF16),
            pltpu.VMEM((2, 4, 8, 2, 128, 128), BF16),
            pltpu.VMEM((16, TK, ROWS), BF16),
            pltpu.VMEM((ROWS, HD), BF16),
            pltpu.VMEM((HD, ROWS), F32),
            pltpu.VMEM((16, 1, ROWS), F32),
            pltpu.VMEM((1, ROWS), F32),
            pltpu.VMEM((1, ROWS), F32),
            pltpu.VMEM((HD, ROWS), F32),
            pltpu.VMEM((4, 8, 2, 128, 128), BF16),
            pltpu.VMEM((2, 8, 128, 128), BF16),
            pltpu.VMEM((2, 8, 2, 128, 128), BF16),
            pltpu.VMEM((2, 4, 4, 2, 128, 128), BF16),
            pltpu.VMEM((4, 2, 128, 128), BF16),
            pltpu.VMEM((8, 2, 128, 128), BF16),
            pltpu.VMEM((4, 128, ROWS), BF16),
            pltpu.VMEM((4, 128, COLS), BF16),
            pltpu.VMEM((2, 8, 80, ROWS), BF16),
            pltpu.VMEM((8, 80, ROWS), BF16),
            pltpu.VMEM((2, 4, 80, ROWS), BF16),
            pltpu.VMEM((128, 128), F32),
            pltpu.VMEM((128, 128), F32),
            pltpu.VMEM((128, 128), F32),
            pltpu.VMEM((128, 1024), F32),
            pltpu.VMEM((128, 1024), BF16),
            pltpu.VMEM((128, 1024), BF16),
            pltpu.VMEM((128, 1024), F32),
            pltpu.VMEM((128, 128), F32),
            pltpu.VMEM((128, 1024), F32),
            pltpu.VMEM((128, 1024), BF16),
            pltpu.VMEM((128, 1024), BF16),
            pltpu.VMEM((8, 1024), F32),
            pltpu.VMEM((8, 1024), F32),
            pltpu.VMEM((8, 16, 1024), BF16),
            pltpu.VMEM((8, 8, 1024), F32),
            pltpu.VMEM((8, 16, 1024), BF16),
            pltpu.VMEM((4, 24, 1024), F32),
            pltpu.VMEM((8, 16, 1024), BF16),
            pltpu.VMEM((8, 16, 1024), BF16),
            pltpu.VMEM((128, 1024), BF16),
            pltpu.VMEM((128, 1024), BF16),
            pltpu.VMEM((128, 1024), BF16),
            pltpu.VMEM((128, 1024), BF16),
            dma, dma((4, 8, 2)), dma((4, 8)),
            dma, dma((16,)), dma((16,)), dma((2, 2)), dma((4, 2)), dma((4,)), dma((8,)),
            dma, dma((4,)), dma, dma((4,)), dma, dma((2, 4)), dma, dma, dma((4, 2)),
            dma((3, 2)), dma((2, 2, 8)), dma((2, 4)), dma((2, 8)), dma,
        ],
        compiler_params=pltpu.CompilerParams(
            collective_id=0, has_side_effects=True, vmem_limit_bytes=58 * 2**20
        ),
    )(query_rows, key_rows, value_rows, mixed_grad, layer_grad,
      state_feed, write_map, read_map, log_decay.T, scan_grad)
    return pl.pallas_call(
        copy_kernel,
        out_shape=shapes,
        in_specs=[vm] * 7,
        out_specs=(vm,) * 7,
    )(*results)


def solution(mesh):
    split = P("ctx", "fsdp")
    return jax.shard_map(
        per_device,
        mesh=mesh,
        in_specs=(split,) * 4 + (P("ctx", None),) + (split,) * 5,
        out_specs=(split,) * 7,
        check_vma=False,
    )
```
